256 devices in a mesh: ctx: 16 (over x, z_hi), head: 8 (over y, core), grp: 2 (over z_lo).
Axes of the slice: x: 4, y: 4, z: 8 (z_hi: 4, z_lo: 2; z = z_hi * 2 + z_lo), core: 2. Of those that a mesh axis runs over, the one named last changes fastest.
Arguments:
- queries: bfloat16 [2, 2048, 8192], P('grp', 'ctx', 'head'), may hold values from -9 to 9
- history_cache: bfloat16 [4, 4096, 8, 256], P(None, 'ctx', 'head'), may hold values from -6 to 6
- fresh_cache: bfloat16 [2, 1024, 8, 256], P('grp', 'ctx', 'head'), may hold values from -6 to 6
- hist_len: int32 [4], replicated, may hold values from 2 to 4096, as said below
- decode_episode: int32 [512], replicated, may hold values from 0 to 3, as said below
Outputs:
- attention: bfloat16 [2, 2048, 8192], P('grp', 'ctx', 'head')
The draws below stay inside these ranges and needn't reach their ends.
Inputs may be any that keep to these rules, and one draw needn't show every extreme that they name: `hist_len`: one episode's length is exactly 4096 in every draw. `decode_episode`: non-decreasing along the decode rows, with the first row in episode 0 and the last in episode 4 - 1.
All inputs are finite; a program needn't handle non-finite values.
Results may differ from the reference program's by a relative error of at most 0.018.
Values may be sent and summed in bfloat16 or wider, within the bound.
A program may use at most 128 MiB of HBM per device.

```python
import math
import jax
import jax.numpy as jnp
from jax import lax

QUERY_HEAD_COUNT = 64
KEY_VALUE_HEADS = 8
HEAD_SIZE = 128
STRETCH_TOKENS = 1024
HISTORY_SLOTS = 4096
EPISODE_TOTAL = 4
STEPS = 4
FRESH_TOKENS = 2048
DEC_ROWS = 512


def draw_queries(key, part):
    key = jax.random.fold_in(key, 11)
    value_rows = jnp.clip(jax.random.normal(key, (2, FRESH_TOKENS, QUERY_HEAD_COUNT, HEAD_SIZE), jnp.float32), -6.0, 6.0)
    return value_rows.reshape(2, FRESH_TOKENS, QUERY_HEAD_COUNT * HEAD_SIZE).astype(jnp.bfloat16)


def draw_history_cache(key, part):
    key = jax.random.fold_in(key, 12)
    value_rows = jnp.clip(jax.random.normal(key, (EPISODE_TOTAL, HISTORY_SLOTS, KEY_VALUE_HEADS, 2 * HEAD_SIZE), jnp.float32), -6.0, 6.0)
    return value_rows.astype(jnp.bfloat16)


def draw_hist_len(key, part):
    key = jax.random.fold_in(key, 13)
    key_len, key_pick = jax.random.split(key)
    lengths = jax.random.randint(key_len, (EPISODE_TOTAL,), 2, HISTORY_SLOTS + 1, jnp.int32)
    chosen = jax.random.randint(key_pick, (), 0, EPISODE_TOTAL, jnp.int32)
    return jnp.where(jnp.arange(EPISODE_TOTAL, dtype=jnp.int32) == chosen, HISTORY_SLOTS, lengths).astype(jnp.int32)


def draw_decode_episode(key, part):
    key = jax.random.fold_in(key, 14)
    cuts = jnp.sort(jax.random.randint(key, (EPISODE_TOTAL - 1,), 1, DEC_ROWS, jnp.int32))
    row_ids = jnp.arange(DEC_ROWS, dtype=jnp.int32)
    return jnp.sum((row_ids[:, None] >= cuts[None, :]).astype(jnp.int32), axis=1).astype(jnp.int32)


def block_levels(stream_key, extent, pieces, smallest, top_value):
    level, own = 1.0, jax.random.fold_in(stream_key, 6)
    for dim, parts in pieces:
        steps = jnp.exp(jax.random.uniform(jax.random.fold_in(own, dim), (parts,), jnp.float32, smallest / len(pieces), top_value / len(pieces)))
        level = level * jnp.repeat(steps, extent[dim] // parts).reshape([-1 if axis == dim else 1 for axis in range(len(extent))])
    return level


def bell_draw(own_key, shape, spread, reach, shards=(), kind=jnp.bfloat16):
    values = jax.random.normal(own_key, shape, jnp.float32) * spread
    if len(shards) > 0:
        values = block_levels(own_key, shape, shards, -0.22, 0.18) * values
    return jnp.clip(values, min=-reach, max=reach).astype(kind)


def setup_inputs(seed: int = 0) -> dict:
    key_of = jax.random.split(jax.random.key(seed), 6)
    return {
        "queries": draw_queries(jax.random.fold_in(key_of[5], 71), 0),
        "history_cache": draw_history_cache(jax.random.fold_in(key_of[5], 71), 0),
        "fresh_cache": bell_draw(key_of[2], (2, STRETCH_TOKENS, KEY_VALUE_HEADS, 2 * HEAD_SIZE), 1.0, 6.0, ((0, 2), (1, 16), (2, 8))),
        "hist_len": draw_hist_len(jax.random.fold_in(key_of[5], 71), 0),
        "decode_episode": draw_decode_episode(jax.random.fold_in(key_of[5], 71), 0),
    }


masked_score = -1e+30

def key_tables(hist_len):
    hist_rows = EPISODE_TOTAL * HISTORY_SLOTS
    slot_ids = jnp.arange(hist_rows + 2 * STRETCH_TOKENS, dtype=jnp.int32)
    is_hist = slot_ids < hist_rows
    key_episode = jnp.where(is_hist, slot_ids // HISTORY_SLOTS, 0).astype(jnp.int32)
    key_place = jnp.where(is_hist, slot_ids % HISTORY_SLOTS, slot_ids - hist_rows).astype(jnp.int32)
    episode_len = hist_len[key_episode]
    return (key_episode, key_place, is_hist, episode_len)

def attend_rows(query_block, episode_block, limit_block, keys_head, values_head, tables):
    key_episode, key_place, is_hist, episode_len = tables
    scores = jnp.einsum('qgd,kd->qgk', query_block.astype(jnp.float32), keys_head.astype(jnp.float32)) / math.sqrt(HEAD_SIZE)
    allowed = (episode_block[:, None] == key_episode[None, :]) & jnp.where(is_hist[None, :], (key_place < episode_len)[None, :], key_place[None, :] <= limit_block[:, None])
    gate = allowed[:, None, :]
    top_score = lax.optimization_barrier(jnp.max(jnp.where(gate, scores, masked_score), axis=-1))
    weights = jnp.where(gate, jnp.exp(scores - top_score[..., None]), 0.0)
    total = lax.optimization_barrier(jnp.sum(weights, axis=-1))
    rounded = weights.astype(jnp.bfloat16)
    summed = jnp.einsum('qgk,kd->qgd', rounded.astype(jnp.float32), values_head.astype(jnp.float32))
    return (summed / total[..., None]).astype(jnp.bfloat16)

def reference(queries, history_cache, fresh_cache, hist_len, decode_episode):
    query_group = QUERY_HEAD_COUNT // KEY_VALUE_HEADS
    tables = key_tables(hist_len)
    every_slot = jnp.concatenate([history_cache.reshape(EPISODE_TOTAL * HISTORY_SLOTS, KEY_VALUE_HEADS, 2 * HEAD_SIZE), fresh_cache.reshape(2 * STRETCH_TOKENS, KEY_VALUE_HEADS, 2 * HEAD_SIZE)], axis=0)
    keys_heads = jnp.transpose(every_slot[:, :, :HEAD_SIZE], (1, 0, 2))
    values_heads = jnp.transpose(every_slot[:, :, HEAD_SIZE:], (1, 0, 2))
    row_ids = jnp.arange(FRESH_TOKENS, dtype=jnp.int32)
    limits = [row_ids, jnp.full((FRESH_TOKENS,), FRESH_TOKENS, jnp.int32)]
    episodes = [jnp.zeros((FRESH_TOKENS,), jnp.int32), decode_episode[row_ids // STEPS]]
    block_span = min(512, FRESH_TOKENS)
    count_of_blocks = FRESH_TOKENS // block_span
    results = []
    for cache_slot_index in range(2):
        heads_of_query = jnp.transpose(queries[cache_slot_index].reshape(FRESH_TOKENS, KEY_VALUE_HEADS, query_group, HEAD_SIZE), (1, 0, 2, 3))
        heads_of_query = heads_of_query.reshape(KEY_VALUE_HEADS, count_of_blocks, block_span, query_group, HEAD_SIZE)
        episode_blocks = episodes[cache_slot_index].reshape(count_of_blocks, block_span)
        limit_blocks = limits[cache_slot_index].reshape(count_of_blocks, block_span)

        def per_head(head_item):
            query_head, keys_head, values_head = head_item

            def per_block(block_item):
                query_block, episode_block, limit_block = block_item
                return attend_rows(query_block, episode_block, limit_block, keys_head, values_head, tables)
            return lax.map(per_block, (query_head, episode_blocks, limit_blocks))
        outputs = lax.map(per_head, (heads_of_query, keys_heads, values_heads))
        outputs = jnp.transpose(outputs, (1, 2, 0, 3, 4)).reshape(FRESH_TOKENS, QUERY_HEAD_COUNT * HEAD_SIZE)
        results.append(outputs)
    return jnp.stack(results, axis=0)
```

```python
import functools
import math

import jax
import jax.numpy as jnp
from jax import lax
from jax.experimental import pallas as pl
from jax.experimental.pallas import tpu as pltpu
from jax.sharding import PartitionSpec as P

MESH = pl.DeviceIdType.MESH
STEPS = 4
RING = 4
EPISODES = 4
HEADS = 8
DIM = 128
SLOTS = 256
HALF = 128
NEW = 64
TILE = 32
LANES = TILE * HEADS
ROWS = 128
TILES = ROWS // TILE
MAIN = RING * TILES
EXTRA = EPISODES - 1
STRETCH = 1024
MASKED = -1e30
SCALE = math.log2(math.e) / math.sqrt(DIM)

OWN, FORWARD, FAR, FAR_FORWARD, PAIR, QUERY, RESULT = 0, 9, 18, 23, 28, 29, 35
COPIES = 47


def kernel(
    q_ref, hist_ref, fresh_ref, len_ref, episode_ref, out_ref,
    hist_d, hist_y, hist_o, fresh_all, q_all,
    acc_o, acc_s, tx_o, tx_s, mid_o, mid_s, fin_o, fin_s, extra_tile,
    send, recv,
):
    ctx = lax.axis_index("ctx")
    grp = lax.axis_index("grp")
    x, k = ctx // RING, ctx % RING
    step = 2 * grp - 1
    k_d = (k + step + RING) % RING
    k_y = (k - step + RING) % RING
    k_o = (k + 2) % RING
    direct = {"ctx": x * RING + k_d, "grp": 1 - grp}
    partner = {"ctx": ctx, "grp": 1 - grp}
    right = {"ctx": (x + 1) % RING * RING + k, "grp": grp}
    left = {"ctx": (x + RING - 1) % RING * RING + k, "grp": grp}

    def remote(number, src, dst, device):
        return pltpu.make_async_remote_copy(
            src_ref=src, dst_ref=dst, send_sem=send.at[number], recv_sem=recv.at[number],
            device_id=device, device_id_type=MESH,
        )

    barrier = pltpu.get_barrier_semaphore()
    for device in (direct, partner, right, left):
        pl.semaphore_signal(barrier, inc=1, device_id=device, device_id_type=MESH)
    pl.semaphore_wait(barrier, 4)

    def half(ref, episode, which):
        return ref.at[episode, pl.ds(pl.multiple_of(which * HALF, HALF), HALF)]

    own, forward = [], []
    for e in range(EPISODES):
        for role in range(2):
            sent = 1 - grp if role == 0 else grp
            had = grp if role == 0 else 1 - grp
            n = 2 * e + role
            own.append(remote(OWN + n, half(hist_ref, e, sent), half(hist_d, e, sent), direct))
            forward.append(remote(FORWARD + n, half(hist_d, e, had), half(hist_y, e, had), partner))
    own.append(remote(OWN + 8, fresh_all.at[0], fresh_all.at[1], direct))
    forward.append(remote(FORWARD + 8, fresh_all.at[1], fresh_all.at[2], partner))
    far, far_forward = [], []
    for e in range(EPISODES):
        far.append(remote(FAR + e, half(hist_y, e, 1 - grp), half(hist_o, e, 1 - grp), direct))
        far_forward.append(remote(FAR_FORWARD + e, half(hist_o, e, grp), half(hist_o, e, grp), partner))
    far.append(remote(FAR + 4, fresh_all.at[2, 1 - grp], fresh_all.at[3, 1 - grp], direct))
    far_forward.append(remote(FAR_FORWARD + 4, fresh_all.at[3, grp], fresh_all.at[3, grp], partner))
    pair = remote(PAIR, fresh_ref, fresh_all.at[0, grp], partner)

    def tiles(slot, part):
        return q_all.at[pl.ds(slot * TILES + part * 2, 2)]

    own_query = [q_ref.at[pl.ds(0, 2)], q_ref.at[pl.ds(2, 2)]]
    queries = [
        remote(QUERY, own_query[0], tiles(1, 0), right),
        remote(QUERY + 1, own_query[1], tiles(2, 1), left),
        remote(QUERY + 2, own_query[1], tiles(1, 1), right),
        remote(QUERY + 3, own_query[0], tiles(2, 0), left),
        remote(QUERY + 4, tiles(1, 0), tiles(3, 0), right),
        remote(QUERY + 5, tiles(2, 1), tiles(3, 1), left),
    ]

    pair.start()
    own[0].start()
    for copy in queries[:4]:
        copy.start()
    for copy in own[1:8]:
        copy.start()
    q_all[0:TILES] = q_ref[...]
    fresh_all[0, grp] = fresh_ref[...]

    lane = lax.broadcasted_iota(jnp.int32, (1, LANES), 1)
    lane_position = lane % TILE
    slot_row = lax.broadcasted_iota(jnp.int32, (SLOTS, LANES), 0)
    new_row = lax.broadcasted_iota(jnp.int32, (NEW, LANES), 0)

    def slot_x(slot):
        return (x + (0, RING - 1, 1, 2)[slot]) % RING

    def decode_row(slot, tile):
        return (slot_x(slot) * RING + k) * (ROWS // STEPS) + tile * (TILE // STEPS)

    def tile_episode(slot, tile):
        return grp * episode_ref[decode_row(slot, tile)]

    for j in range(EXTRA):
        extra_tile[j] = 0
    for slot in range(RING):
        for tile in range(TILES):
            low = tile_episode(slot, tile)
            high = grp * episode_ref[decode_row(slot, tile) + TILE // STEPS - 1]
            for j in range(EXTRA):
                hit = (low < j + 1) & (high >= j + 1)
                extra_tile[j] = jnp.where(hit, slot * TILES + tile, extra_tile[j])

    def stack_heads(block):
        return jnp.concatenate([block[:, h * DIM:(h + 1) * DIM] for h in range(HEADS)], axis=0)

    def scores(keys, block):
        return lax.dot_general(keys, stack_heads(block), (((1,), (1,)), ((), ())), preferred_element_type=jnp.float32)

    def update(i, s, values, first):
        top = jnp.max(s, axis=0, keepdims=True)
        if not first:
            top_old = acc_s[i, 0:1]
            top = jnp.maximum(top, top_old)
        p = jnp.exp2(s * SCALE - top * SCALE)
        total = jnp.sum(p, axis=0, keepdims=True)
        summed = lax.dot_general(
            values, p.astype(jnp.bfloat16), (((0,), (0,)), ((), ())), preferred_element_type=jnp.float32
        )
        if not first:
            rescale = jnp.exp2((top_old - top) * SCALE)
            total = total + acc_s[i, 1:2] * rescale
            summed = summed + acc_o[i] * rescale
        acc_s[i, 0:1] = top
        acc_s[i, 1:2] = total
        acc_o[i] = summed

    def history(ref, block, i, query, episode, first):
        allowed = slot_row < len_ref[episode] - (x * RING + block) * SLOTS
        s = jnp.where(allowed, scores(ref[episode, :, 0:DIM], query), MASKED)
        update(i, s, ref[episode, :, DIM:2 * DIM], first)

    def history_slot(ref, block, slot, first=False):
        def body(tile, carry):
            i = slot * TILES + tile
            history(ref, block, i, q_all[i], tile_episode(slot, tile), first)
            return carry

        lax.fori_loop(0, TILES, body, 0)

    def history_extra(ref, block, first=False):
        def body(j, carry):
            history(ref, block, MAIN + j, q_all[extra_tile[j]], j + 1, first)
            return carry

        lax.fori_loop(0, EXTRA, body, 0)

    def new_tokens(slot):
        def body(tile, carry):
            i = slot * TILES + tile
            prefill = (slot_x(slot) * RING + k) * ROWS + tile * TILE + lane_position
            decode = jnp.where(tile_episode(slot, tile) == 0, 2 * STRETCH, -1)
            limit = jnp.where(grp == 0, prefill, decode)
            keys = fresh_all[:, :, :, 0:DIM].reshape(RING * 2 * NEW, DIM)
            s = scores(keys, q_all[i])
            parts = []
            for part in range(2 * RING):
                block = (k, k_d, k_y, k_o)[part // 2]
                base = part % 2 * STRETCH + (x * RING + block) * NEW
                parts.append(jnp.where(new_row <= limit - base, s[part * NEW:(part + 1) * NEW], MASKED))
            update(i, jnp.concatenate(parts, axis=0), fresh_all[:, :, :, DIM:2 * DIM].reshape(RING * 2 * NEW, DIM), False)
            return carry

        lax.fori_loop(0, TILES, body, 0)

    def hand_on(received, onward):
        received.wait_recv()
        onward.start()

    history_slot(hist_ref, k, 0, True)
    pair.wait_recv()
    own[8].start()
    hand_on(queries[0], queries[4])
    hand_on(queries[1], queries[5])
    for n in (0, 1):
        hand_on(own[n], forward[n])
    queries[2].wait_recv()
    history_slot(hist_ref, k, 1, True)
    queries[3].wait_recv()
    hand_on(own[2], forward[2])
    history_slot(hist_ref, k, 2, True)
    for n in (3, 4):
        hand_on(own[n], forward[n])
    queries[4].wait_recv()
    queries[5].wait_recv()
    history_slot(hist_ref, k, 3, True)
    hand_on(own[5], forward[5])
    history_extra(hist_ref, k, True)
    for n in (6, 7, 8):
        hand_on(own[n], forward[n])

    for slot in range(RING):
        hand_on(forward[2 * slot], far[slot])
        history_slot(hist_d, k_d, slot)
    history_extra(hist_d, k_d)
    hand_on(forward[8], far[4])

    for n in (1, 3, 5, 7):
        forward[n].wait_recv()
    for slot in range(RING):
        hand_on(far[slot], far_forward[slot])
        history_slot(hist_y, k_y, slot)
    history_extra(hist_y, k_y)
    hand_on(far[4], far_forward[4])

    far_forward[4].wait_recv()
    for slot in range(RING):
        new_tokens(slot)
    for e in range(EPISODES):
        far_forward[e].wait_recv()
    history_extra(hist_o, k_o)

    def state(slot, tile):
        i = slot * TILES + tile
        top, total, summed = acc_s[i, 0:1], acc_s[i, 1:2], acc_o[i]
        first = tile_episode(slot, tile)
        row_episode = jnp.zeros((1, LANES), jnp.int32)
        for r in range(TILE // STEPS):
            row_episode = jnp.where(
                lane_position // STEPS == r, grp * episode_ref[decode_row(slot, tile) + r], row_episode
            )
        for j in range(EXTRA):
            other = (row_episode == j + 1) & (first != j + 1)
            top = jnp.where(other, acc_s[MAIN + j, 0:1], top)
            total = jnp.where(other, acc_s[MAIN + j, 1:2], total)
            summed = jnp.where(other, acc_o[MAIN + j], summed)
        return top, total, summed

    def merge(one, two):
        top = jnp.maximum(one[0], two[0])
        a, b = jnp.exp2((one[0] - top) * SCALE), jnp.exp2((two[0] - top) * SCALE)
        return top, one[1] * a + two[1] * b, one[2] * a + two[2] * b

    def load(o_ref, s_ref, tile):
        return s_ref[2 * tile:2 * tile + 1], s_ref[2 * tile + 1:2 * tile + 2], o_ref[tile].astype(jnp.float32)

    def result(number, slot, part, into_o, into_s, device):
        n = (slot - 1) * 2 + part
        return (
            remote(RESULT + 2 * number, tx_o.at[n], into_o, device),
            remote(RESULT + 2 * number + 1, tx_s.at[n], into_s, device),
        )

    results = [
        result(0, 3, 0, mid_o.at[0], mid_s.at[0], right),
        result(1, 3, 1, mid_o.at[1], mid_s.at[1], left),
        result(2, 2, 1, fin_o.at[0, 1], fin_s.at[0, 1], right),
        result(3, 1, 0, fin_o.at[1, 0], fin_s.at[1, 0], left),
        result(4, 2, 0, fin_o.at[0, 0], fin_s.at[0, 0], right),
        result(5, 1, 1, fin_o.at[1, 1], fin_s.at[1, 1], left),
    ]

    def pack(slot, part, incoming=None):
        n = (slot - 1) * 2 + part
        for t in range(2):
            now = state(slot, part * 2 + t)
            if incoming is not None:
                now = merge(now, load(mid_o.at[incoming], mid_s.at[incoming], t))
            tx_s[n, 2 * t:2 * t + 1] = now[0]
            tx_s[n, 2 * t + 1:2 * t + 2] = now[1]
            tx_o[n, t] = now[2].astype(jnp.bfloat16)

    def ship(number):
        for copy in results[number]:
            copy.start()

    def arrive(number):
        for copy in results[number]:
            copy.wait_recv()

    tx_s[...] = jnp.zeros_like(tx_s)
    history_slot(hist_o, k_o, 3)
    pack(3, 0)
    ship(0)
    pack(3, 1)
    ship(1)
    history_slot(hist_o, k_o, 2)
    pack(2, 1)
    ship(2)
    history_slot(hist_o, k_o, 1)
    pack(1, 0)
    ship(3)
    arrive(0)
    pack(2, 0, 0)
    ship(4)
    arrive(1)
    pack(1, 1, 1)
    ship(5)
    history_slot(hist_o, k_o, 0)

    for number in (2, 3, 4, 5):
        arrive(number)
    for tile in range(TILES):
        now = state(0, tile)
        for side in range(2):
            now = merge(now, load(fin_o.at[side, tile // 2], fin_s.at[side, tile // 2], tile % 2))
        whole = (now[2] * (1.0 / now[1])).T.astype(jnp.bfloat16)
        for h in range(HEADS):
            out_ref[tile, :, h * DIM:(h + 1) * DIM] = whole[h * TILE:(h + 1) * TILE]

    sent = own + forward + far + far_forward + [pair] + queries
    for copy in sent + [c for both in results for c in both]:
        copy.wait_send()


def local(queries, history_cache, fresh_cache, hist_len, decode_episode):
    vmem = pl.BlockSpec(memory_space=pltpu.VMEM)
    smem = pl.BlockSpec(memory_space=pltpu.SMEM)
    bf16, f32 = jnp.bfloat16, jnp.float32
    block = pltpu.VMEM((EPISODES, SLOTS, 2 * DIM), bf16)
    out = pl.pallas_call(
        kernel,
        out_shape=jax.ShapeDtypeStruct((TILES, TILE, HEADS * DIM), bf16),
        in_specs=[vmem, vmem, vmem, smem, smem],
        out_specs=vmem,
        scratch_shapes=[
            block,
            block,
            block,
            pltpu.VMEM((RING, 2, NEW, 2 * DIM), bf16),
            pltpu.VMEM((MAIN, TILE, HEADS * DIM), bf16),
            pltpu.VMEM((MAIN + EXTRA, DIM, LANES), f32),
            pltpu.VMEM((MAIN + EXTRA, 8, LANES), f32),
            pltpu.VMEM((6, 2, DIM, LANES), bf16),
            pltpu.VMEM((6, 8, LANES), f32),
            pltpu.VMEM((2, 2, DIM, LANES), bf16),
            pltpu.VMEM((2, 8, LANES), f32),
            pltpu.VMEM((2, 2, 2, DIM, LANES), bf16),
            pltpu.VMEM((2, 2, 8, LANES), f32),
            pltpu.SMEM((EXTRA,), jnp.int32),
            pltpu.SemaphoreType.DMA((COPIES,)),
            pltpu.SemaphoreType.DMA((COPIES,)),
        ],
        compiler_params=pltpu.CompilerParams(
            collective_id=0, has_side_effects=True, vmem_limit_bytes=40 * 1024 * 1024
        ),
    )(
        queries.reshape(TILES, TILE, HEADS * DIM),
        history_cache.reshape(EPISODES, SLOTS, 2 * DIM),
        fresh_cache.reshape(NEW, 2 * DIM),
        hist_len,
        decode_episode,
    )
    return out.reshape(1, ROWS, HEADS * DIM)


def solution(mesh):
    placed = (
        P("grp", "ctx", "head"),
        P(None, "ctx", "head", None),
        P("grp", "ctx", "head", None),
        P(),
        P(),
    )
    return jax.shard_map(
        local, mesh=mesh, in_specs=placed, out_specs=P("grp", "ctx", "head"), check_vma=False
    )
```

```python
import functools
import math

import jax
import jax.numpy as jnp
from jax import lax
from jax.experimental import pallas as pl
from jax.experimental.pallas import tpu as pltpu
from jax.sharding import PartitionSpec as P

MESH = pl.DeviceIdType.MESH
STEPS = 4
RING = 4
EPISODES = 4
HEADS = 8
DIM = 128
SLOTS = 256
HALF = 128
NEW = 64
TILE = 32
LANES = TILE * HEADS
ROWS = 128
TILES = ROWS // TILE
MAIN = RING * TILES
EXTRA = EPISODES - 1
STRETCH = 1024
MASKED = -1e30
SCALE = math.log2(math.e) / math.sqrt(DIM)

OWN, FORWARD, FAR, FAR_FORWARD, PAIR, QUERY, RESULT = 0, 9, 18, 23, 28, 29, 35
COPIES = 47


def kernel(
    q_ref, hist_ref, fresh_ref, len_in, episode_in, out_ref,
    len_ref, episode_ref, hist_own, hist_d, hist_y, hist_o, fresh_all, q_all,
    acc_o, acc_s, tx_o, tx_s, mid_o, mid_s, fin_o, fin_s, extra_tile,
    send, recv, inside,
):
    ctx = lax.axis_index("ctx")
    grp = lax.axis_index("grp")
    x, k = ctx // RING, ctx % RING
    step = 2 * grp - 1
    k_d = (k + step + RING) % RING
    k_y = (k - step + RING) % RING
    k_o = (k + 2) % RING
    direct = {"ctx": x * RING + k_d, "grp": 1 - grp}
    partner = {"ctx": ctx, "grp": 1 - grp}
    right = {"ctx": (x + 1) % RING * RING + k, "grp": grp}
    left = {"ctx": (x + RING - 1) % RING * RING + k, "grp": grp}

    def remote(number, src, dst, device):
        return pltpu.make_async_remote_copy(
            src_ref=src, dst_ref=dst, send_sem=send.at[number], recv_sem=recv.at[number],
            device_id=device, device_id_type=MESH,
        )

    local_copies = [
        pltpu.make_async_copy(src, dst, inside.at[n])
        for n, (src, dst) in enumerate([
            (len_in, len_ref), (episode_in, episode_ref), (fresh_ref, fresh_all.at[0, grp]),
            (q_ref, q_all.at[pl.ds(0, TILES)]), (hist_ref, hist_own),
        ])
    ]
    for copy in local_copies:
        copy.start()

    barrier = pltpu.get_barrier_semaphore()
    for device in (direct, partner, right, left):
        pl.semaphore_signal(barrier, inc=1, device_id=device, device_id_type=MESH)
    pl.semaphore_wait(barrier, 4)

    def half(ref, episode, which):
        return ref.at[episode, pl.ds(pl.multiple_of(which * HALF, HALF), HALF)]

    own, forward = [], []
    for e in range(EPISODES):
        for role in range(2):
            sent = 1 - grp if role == 0 else grp
            had = grp if role == 0 else 1 - grp
            n = 2 * e + role
            own.append(remote(OWN + n, half(hist_ref, e, sent), half(hist_d, e, sent), direct))
            forward.append(remote(FORWARD + n, half(hist_d, e, had), half(hist_y, e, had), partner))
    own.append(remote(OWN + 8, fresh_all.at[0], fresh_all.at[1], direct))
    forward.append(remote(FORWARD + 8, fresh_all.at[1], fresh_all.at[2], partner))
    far, far_forward = [], []
    for e in range(EPISODES):
        far.append(remote(FAR + e, half(hist_y, e, 1 - grp), half(hist_o, e, 1 - grp), direct))
        far_forward.append(remote(FAR_FORWARD + e, half(hist_o, e, grp), half(hist_o, e, grp), partner))
    far.append(remote(FAR + 4, fresh_all.at[2, 1 - grp], fresh_all.at[3, 1 - grp], direct))
    far_forward.append(remote(FAR_FORWARD + 4, fresh_all.at[3, grp], fresh_all.at[3, grp], partner))
    pair = remote(PAIR, fresh_ref, fresh_all.at[0, grp], partner)

    def tiles(slot, part):
        return q_all.at[pl.ds(slot * TILES + part * 2, 2)]

    own_query = [q_ref.at[pl.ds(0, 2)], q_ref.at[pl.ds(2, 2)]]
    queries = [
        remote(QUERY, own_query[0], tiles(1, 0), right),
        remote(QUERY + 1, own_query[1], tiles(2, 1), left),
        remote(QUERY + 2, own_query[1], tiles(1, 1), right),
        remote(QUERY + 3, own_query[0], tiles(2, 0), left),
        remote(QUERY + 4, tiles(1, 0), tiles(3, 0), right),
        remote(QUERY + 5, tiles(2, 1), tiles(3, 1), left),
    ]

    pair.start()
    own[0].start()
    for copy in queries[:4]:
        copy.start()
    own[1].start()
    for copy in local_copies:
        copy.wait()

    lane = lax.broadcasted_iota(jnp.int32, (1, LANES), 1)
    lane_position = lane % TILE
    slot_row = lax.broadcasted_iota(jnp.int32, (SLOTS, LANES), 0)
    new_row = lax.broadcasted_iota(jnp.int32, (NEW, LANES), 0)

    def slot_x(slot):
        return (x + (0, RING - 1, 1, 2)[slot]) % RING

    def decode_row(slot, tile):
        return (slot_x(slot) * RING + k) * (ROWS // STEPS) + tile * (TILE // STEPS)

    def tile_episode(slot, tile):
        return grp * episode_ref[decode_row(slot, tile)]

    for j in range(EXTRA):
        extra_tile[j] = 0
    for slot in range(RING):
        for tile in range(TILES):
            low = tile_episode(slot, tile)
            high = grp * episode_ref[decode_row(slot, tile) + TILE // STEPS - 1]
            for j in range(EXTRA):
                hit = (low < j + 1) & (high >= j + 1)
                extra_tile[j] = jnp.where(hit, slot * TILES + tile, extra_tile[j])

    def stack_heads(block):
        return jnp.concatenate([block[:, h * DIM:(h + 1) * DIM] for h in range(HEADS)], axis=0)

    def scores(keys, block):
        return lax.dot_general(keys, stack_heads(block), (((1,), (1,)), ((), ())), preferred_element_type=jnp.float32)

    def update(items, all_scores, all_values, first):
        tops = [jnp.max(s, axis=0, keepdims=True) for s in all_scores]
        if not first:
            olds = [(acc_s[i, 0:1], acc_s[i, 1:2]) for i in items]
            tops = [jnp.maximum(top, old[0]) for top, old in zip(tops, olds)]
        weights = [jnp.exp2(s * SCALE - top * SCALE) for s, top in zip(all_scores, tops)]
        totals = [jnp.sum(p, axis=0, keepdims=True) for p in weights]
        sums = [
            lax.dot_general(
                values, p.astype(jnp.bfloat16), (((0,), (0,)), ((), ())), preferred_element_type=jnp.float32
            )
            for values, p in zip(all_values, weights)
        ]
        if not first:
            rescales = [jnp.exp2((old[0] - top) * SCALE) for old, top in zip(olds, tops)]
            totals = [total + old[1] * r for total, old, r in zip(totals, olds, rescales)]
            sums = [summed + acc_o[i] * r for i, summed, r in zip(items, sums, rescales)]
        for i, top, total, summed in zip(items, tops, totals, sums):
            acc_s[i, 0:1] = top
            acc_s[i, 1:2] = total
            acc_o[i] = summed

    def history(ref, block, items, first=False):
        all_scores, all_values = [], []
        for i in items:
            if i < MAIN:
                query, episode = q_all[i], tile_episode(i // TILES, i % TILES)
            else:
                query, episode = q_all[extra_tile[i - MAIN]], i - MAIN + 1
            allowed = slot_row < len_ref[episode] - (x * RING + block) * SLOTS
            all_scores.append(jnp.where(allowed, scores(ref[episode, :, 0:DIM], query), MASKED))
            all_values.append(ref[episode, :, DIM:2 * DIM])
        update(items, all_scores, all_values, first)

    def new_tokens(items):
        keys = fresh_all[:, :, :, 0:DIM].reshape(RING * 2 * NEW, DIM)
        values = fresh_all[:, :, :, DIM:2 * DIM].reshape(RING * 2 * NEW, DIM)
        all_scores = []
        for i in items:
            slot, tile = i // TILES, i % TILES
            prefill = (slot_x(slot) * RING + k) * ROWS + tile * TILE + lane_position
            decode = jnp.where(tile_episode(slot, tile) == 0, 2 * STRETCH, -1)
            limit = jnp.where(grp == 0, prefill, decode)
            s = scores(keys, q_all[i])
            parts = []
            for part in range(2 * RING):
                block = (k, k_d, k_y, k_o)[part // 2]
                base = part % 2 * STRETCH + (x * RING + block) * NEW
                parts.append(jnp.where(new_row <= limit - base, s[part * NEW:(part + 1) * NEW], MASKED))
            all_scores.append(jnp.concatenate(parts, axis=0))
        update(items, all_scores, [values] * len(items), False)

    def hand_on(received, onward):
        received.wait_recv()
        onward.start()

    def span(first, last):
        return list(range(first, last))

    def next_own(n):
        if n < 8:
            own[n].start()

    history(hist_own, k, span(0, 4), True)
    pair.wait_recv()
    own[8].start()
    own[2].start()
    hand_on(queries[0], queries[4])
    hand_on(queries[1], queries[5])
    hand_on(own[0], forward[0])
    next_own(3)
    hand_on(own[1], forward[1])
    next_own(4)
    hand_on(own[8], forward[8])
    next_own(5)
    queries[2].wait_recv()
    queries[3].wait_recv()
    history(hist_own, k, span(4, 12), True)
    hand_on(own[2], forward[2])
    next_own(6)
    hand_on(forward[8], far[4])
    hand_on(own[3], forward[3])
    next_own(7)
    queries[4].wait_recv()
    queries[5].wait_recv()
    history(hist_own, k, span(12, 19), True)
    hand_on(own[4], forward[4])
    hand_on(forward[0], far[0])
    hand_on(own[5], forward[5])
    hand_on(forward[2], far[1])
    hand_on(far[4], far_forward[4])
    hand_on(own[6], forward[6])
    hand_on(forward[4], far[2])
    far_forward[4].wait_recv()
    new_tokens(span(0, 4))
    hand_on(own[7], forward[7])
    new_tokens(span(4, 8))
    hand_on(forward[6], far[3])
    hand_on(far[0], far_forward[0])
    new_tokens(span(8, 12))
    hand_on(far[1], far_forward[1])
    new_tokens(span(12, 16))
    hand_on(far[2], far_forward[2])
    history(hist_d, k_d, span(0, 8))
    hand_on(far[3], far_forward[3])
    history(hist_d, k_d, span(8, 19))
    for n in (1, 3, 5, 7):
        forward[n].wait_recv()
    history(hist_y, k_y, span(0, 8))
    history(hist_y, k_y, span(8, 19))
    for e in range(EPISODES):
        far_forward[e].wait_recv()

    def state(slot, tile):
        i = slot * TILES + tile
        top, total, summed = acc_s[i, 0:1], acc_s[i, 1:2], acc_o[i]
        first = tile_episode(slot, tile)
        row_episode = jnp.zeros((1, LANES), jnp.int32)
        for r in range(TILE // STEPS):
            row_episode = jnp.where(
                lane_position // STEPS == r, grp * episode_ref[decode_row(slot, tile) + r], row_episode
            )
        for j in range(EXTRA):
            other = (row_episode == j + 1) & (first != j + 1)
            top = jnp.where(other, acc_s[MAIN + j, 0:1], top)
            total = jnp.where(other, acc_s[MAIN + j, 1:2], total)
            summed = jnp.where(other, acc_o[MAIN + j], summed)
        return top, total, summed

    def merge(one, two):
        top = jnp.maximum(one[0], two[0])
        a, b = jnp.exp2((one[0] - top) * SCALE), jnp.exp2((two[0] - top) * SCALE)
        return top, one[1] * a + two[1] * b, one[2] * a + two[2] * b

    def load(o_ref, s_ref, tile):
        return s_ref[2 * tile:2 * tile + 1], s_ref[2 * tile + 1:2 * tile + 2], o_ref[tile].astype(jnp.float32)

    def result(number, slot, part, into_o, into_s, device):
        n = (slot - 1) * 2 + part
        return (
            remote(RESULT + 2 * number, tx_o.at[n], into_o, device),
            remote(RESULT + 2 * number + 1, tx_s.at[n], into_s, device),
        )

    results = [
        result(0, 3, 0, mid_o.at[0], mid_s.at[0], right),
        result(1, 3, 1, mid_o.at[1], mid_s.at[1], left),
        result(2, 2, 1, fin_o.at[0, 1], fin_s.at[0, 1], right),
        result(3, 1, 0, fin_o.at[1, 0], fin_s.at[1, 0], left),
        result(4, 2, 0, fin_o.at[0, 0], fin_s.at[0, 0], right),
        result(5, 1, 1, fin_o.at[1, 1], fin_s.at[1, 1], left),
    ]

    def pack(slot, part, incoming=None):
        n = (slot - 1) * 2 + part
        for t in range(2):
            now = state(slot, part * 2 + t)
            if incoming is not None:
                now = merge(now, load(mid_o.at[incoming], mid_s.at[incoming], t))
            tx_s[n, 2 * t:2 * t + 1] = now[0]
            tx_s[n, 2 * t + 1:2 * t + 2] = now[1]
            tx_o[n, t] = now[2].astype(jnp.bfloat16)

    def ship(number):
        for copy in results[number]:
            copy.start()

    def arrive(number):
        for copy in results[number]:
            copy.wait_recv()

    tx_s[...] = jnp.zeros_like(tx_s)
    history(hist_o, k_o, span(12, 19))
    pack(3, 0)
    ship(0)
    pack(3, 1)
    ship(1)
    history(hist_o, k_o, span(4, 12))
    pack(2, 1)
    ship(2)
    pack(1, 0)
    ship(3)
    arrive(0)
    pack(2, 0, 0)
    ship(4)
    arrive(1)
    pack(1, 1, 1)
    ship(5)
    history(hist_o, k_o, span(0, 4))

    for number in (2, 3, 4, 5):
        arrive(number)
    for tile in range(TILES):
        now = state(0, tile)
        for side in range(2):
            now = merge(now, load(fin_o.at[side, tile // 2], fin_s.at[side, tile // 2], tile % 2))
        whole = (now[2] * (1.0 / now[1])).T.astype(jnp.bfloat16)
        for h in range(HEADS):
            out_ref[tile, :, h * DIM:(h + 1) * DIM] = whole[h * TILE:(h + 1) * TILE]

    sent = own + forward + far + far_forward + [pair] + queries
    for copy in sent + [c for both in results for c in both]:
        copy.wait_send()


def local(queries, history_cache, fresh_cache, hist_len, decode_episode):
    vmem = pl.BlockSpec(memory_space=pltpu.VMEM)
    bf16, f32 = jnp.bfloat16, jnp.float32
    block = pltpu.VMEM((EPISODES, SLOTS, 2 * DIM), bf16)
    out = pl.pallas_call(
        kernel,
        out_shape=jax.ShapeDtypeStruct((TILES, TILE, HEADS * DIM), bf16),
        in_specs=[pl.BlockSpec(memory_space=pl.ANY)] * 5,
        out_specs=vmem,
        scratch_shapes=[
            pltpu.SMEM((EPISODES,), jnp.int32),
            pltpu.SMEM((512,), jnp.int32),
            block,
            block,
            block,
            block,
            pltpu.VMEM((RING, 2, NEW, 2 * DIM), bf16),
            pltpu.VMEM((MAIN, TILE, HEADS * DIM), bf16),
            pltpu.VMEM((MAIN + EXTRA, DIM, LANES), f32),
            pltpu.VMEM((MAIN + EXTRA, 8, LANES), f32),
            pltpu.VMEM((6, 2, DIM, LANES), bf16),
            pltpu.VMEM((6, 8, LANES), f32),
            pltpu.VMEM((2, 2, DIM, LANES), bf16),
            pltpu.VMEM((2, 8, LANES), f32),
            pltpu.VMEM((2, 2, 2, DIM, LANES), bf16),
            pltpu.VMEM((2, 2, 8, LANES), f32),
            pltpu.SMEM((EXTRA,), jnp.int32),
            pltpu.SemaphoreType.DMA((COPIES,)),
            pltpu.SemaphoreType.DMA((COPIES,)),
            pltpu.SemaphoreType.DMA((5,)),
        ],
        compiler_params=pltpu.CompilerParams(
            collective_id=0, has_side_effects=True, vmem_limit_bytes=56 * 1024 * 1024
        ),
    )(
        queries.reshape(TILES, TILE, HEADS * DIM),
        history_cache.reshape(EPISODES, SLOTS, 2 * DIM),
        fresh_cache.reshape(NEW, 2 * DIM),
        hist_len,
        decode_episode,
    )
    return out.reshape(1, ROWS, HEADS * DIM)


def solution(mesh):
    placed = (
        P("grp", "ctx", "head"),
        P(None, "ctx", "head", None),
        P("grp", "ctx", "head", None),
        P(),
        P(),
    )
    return jax.shard_map(
        local, mesh=mesh, in_specs=placed, out_specs=P("grp", "ctx", "head"), check_vma=False
    )
```

```python
import functools
import math

import jax
import jax.numpy as jnp
from jax import lax
from jax.experimental import pallas as pl
from jax.experimental.pallas import tpu as pltpu
from jax.sharding import PartitionSpec as P

MESH = pl.DeviceIdType.MESH
STEPS = 4
RING = 4
EPISODES = 4
HEADS = 8
DIM = 128
SLOTS = 256
HALF = 128
NEW = 64
TILE = 32
LANES = TILE * HEADS
ROWS = 128
TILES = ROWS // TILE
MAIN = RING * TILES
EXTRA = EPISODES - 1
STRETCH = 1024
MASKED = -1e30
SCALE = math.log2(math.e) / math.sqrt(DIM)

FROM_RIGHT, FROM_LEFT, FAR_LOW, FAR_HIGH, PAIR, QUERY, RESULT = 0, 9, 18, 23, 28, 29, 35
RELAY = 47
COPIES = 54


def kernel(
    q_ref, hist_ref, fresh_ref, len_in, episode_in, out_ref,
    len_ref, episode_ref, hist_own, hist_d, hist_y, hist_o, fresh_all, q_all,
    acc_o, acc_s, tx_o, tx_s, mid_o, mid_s, fin_o, fin_s, extra_tile,
    send, recv, inside,
):
    ctx = lax.axis_index("ctx")
    grp = lax.axis_index("grp")
    core = lax.axis_index("head") % 2
    x, k = ctx // RING, ctx % RING
    buffers = (hist_own, hist_d, hist_y, hist_o)

    def place(x_at, k_at):
        return (x_at + RING) % RING * RING + (k_at + RING) % RING

    direct = {"ctx": place(x, k + 2 * grp - 1), "grp": 1 - grp}
    partner = {"ctx": ctx, "grp": 1 - grp}
    x_right, x_left = {"ctx": place(x + 1, k)}, {"ctx": place(x - 1, k)}
    z_right, z_left = {"ctx": place(x, k + 1)}, {"ctx": place(x, k - 1)}

    def remote(number, src, dst, device, sender=None):
        return pltpu.make_async_remote_copy(
            src_ref=src, dst_ref=dst, send_sem=send.at[number if sender is None else sender], recv_sem=recv.at[number],
            device_id=device, device_id_type=MESH,
        )

    local_copies = [
        pltpu.make_async_copy(src, dst, inside.at[n])
        for n, (src, dst) in enumerate([
            (len_in, len_ref), (episode_in, episode_ref), (fresh_ref, fresh_all.at[0, grp]),
            (q_ref, q_all.at[pl.ds(0, TILES)]), (hist_ref, hist_own),
        ])
    ]
    for copy in local_copies:
        copy.start()

    barrier = pltpu.get_barrier_semaphore()

    def greet(device):
        pl.semaphore_signal(barrier, inc=1, device_id=device, device_id_type=MESH)

    greet(partner)
    greet(x_right)
    greet(x_left)

    @pl.when(core == 0)
    def _():
        greet(direct)

    @pl.when(core + grp > 0)
    def _():
        greet(z_right)
        greet(z_left)

    pl.semaphore_wait(barrier, jnp.where(core == 1, 5, 4 + 2 * grp))
    for copy in local_copies:
        copy.wait()

    lane = lax.broadcasted_iota(jnp.int32, (1, LANES), 1)
    lane_position = lane % TILE
    slot_row = lax.broadcasted_iota(jnp.int32, (SLOTS, LANES), 0)
    new_row = lax.broadcasted_iota(jnp.int32, (NEW, LANES), 0)

    def half(ref, episode, which):
        if not isinstance(which, int):
            which = pl.multiple_of(which * HALF, HALF)
        else:
            which = which * HALF
        return ref.at[episode, pl.ds(which, HALF)]

    def stack_heads(block):
        return jnp.concatenate([block[:, h * DIM:(h + 1) * DIM] for h in range(HEADS)], axis=0)

    def scores(keys, block):
        return lax.dot_general(keys, stack_heads(block), (((1,), (1,)), ((), ())), preferred_element_type=jnp.float32)

    def update(items, all_scores, all_values, first):
        tops = []
        for parts in all_scores:
            top = jnp.max(parts[0], axis=0, keepdims=True)
            for s in parts[1:]:
                top = jnp.maximum(top, jnp.max(s, axis=0, keepdims=True))
            tops.append(top)
        if not first:
            olds = [(acc_s[i, 0:1], acc_s[i, 1:2]) for i in items]
            tops = [jnp.maximum(top, old[0]) for top, old in zip(tops, olds)]
        weights = [[jnp.exp2(s * SCALE - top * SCALE) for s in parts] for parts, top in zip(all_scores, tops)]
        totals = [sum(jnp.sum(p, axis=0, keepdims=True) for p in parts) for parts in weights]
        sums = [
            sum(
                lax.dot_general(v, p.astype(jnp.bfloat16), (((0,), (0,)), ((), ())), preferred_element_type=jnp.float32)
                for v, p in zip(values, parts)
            )
            for values, parts in zip(all_values, weights)
        ]
        if not first:
            rescales = [jnp.exp2((old[0] - top) * SCALE) for old, top in zip(olds, tops)]
            totals = [total + old[1] * r for total, old, r in zip(totals, olds, rescales)]
            sums = [summed + acc_o[i] * r for i, summed, r in zip(items, sums, rescales)]
        for i, top, total, summed in zip(items, tops, totals, sums):
            acc_s[i, 0:1] = top
            acc_s[i, 1:2] = total
            acc_o[i] = summed

    def merge(one, two):
        top = jnp.maximum(one[0], two[0])
        a, b = jnp.exp2((one[0] - top) * SCALE), jnp.exp2((two[0] - top) * SCALE)
        return top, one[1] * a + two[1] * b, one[2] * a + two[2] * b

    def load(o_ref, s_ref, tile):
        return s_ref[2 * tile:2 * tile + 1], s_ref[2 * tile + 1:2 * tile + 2], o_ref[tile].astype(jnp.float32)

    def span(first, last):
        return list(range(first, last))

    class Copy:
        def __init__(self, number, ends, receives, sender=None):
            self.number, self.ends, self.receives, self.sender = number, ends, receives, sender

        def each(self, wanted, act):
            if all(wanted) and self.ends[0] is self.ends[1]:
                act(0)
                return
            for c in range(2):
                if wanted[c]:
                    pl.when(core == c)(functools.partial(act, c))

        def of(self, ends):
            return remote(self.number, *ends, self.sender)

        def start(self):
            self.each([e is not None for e in self.ends], lambda c: self.of(self.ends[c]).start())

        def wait_send(self):
            self.each([e is not None for e in self.ends], lambda c: self.of(self.ends[c]).wait_send())

        def wait_recv(self):
            ends = self.ends[0] or self.ends[1]
            if all(self.receives):
                self.of(ends).wait_recv()
            else:
                self.each(self.receives, lambda c: self.of(ends).wait_recv())

    def program(prefill):
        me = 0 if prefill else 1
        def either(one, two):
            return {"ctx": jnp.where(core == 1, one["ctx"], two["ctx"])}

        if prefill:
            kv_right, kv_left, q_right, q_left = z_right, z_left, x_right, x_left
            blocks = [place(x, k + off) for off in (0, 1, -1, 2)]
        else:
            kv_right, kv_left = either(x_right, z_right), either(x_left, z_left)
            q_right, q_left = either(z_right, x_right), either(z_left, x_left)
            blocks = [jnp.where(core == 1, place(x + off, k), place(x, k + off)) for off in (0, 1, -1, 2)]

        def row_block(slot):
            off = (0, -1, 1, 2)[slot]
            if prefill:
                return place(x + off, k)
            return jnp.where(core == 1, place(x, k + off), place(x + off, k))

        from_right, from_left, far_low, far_high, relays = {}, {}, {}, {}, {}
        for e in list(range(EPISODES)) + ["new"]:
            ring = not prefill or e in (0, "new")
            n = 2 * EPISODES if e == "new" else 2 * e
            f = EPISODES if e == "new" else e
            for h in range(2 if e != "new" else 1):
                if e == "new":
                    here, right, left = fresh_all.at[0], fresh_all.at[1], fresh_all.at[2]
                    low, to_low = fresh_all.at[1, 0], fresh_all.at[3, 0]
                    high, to_high = fresh_all.at[2, 1], fresh_all.at[3, 1]
                else:
                    here, right, left = half(hist_ref, e, h), half(hist_d, e, h), half(hist_y, e, h)
                    low, to_low = half(hist_d, e, 0), half(hist_o, e, 0)
                    high, to_high = half(hist_y, e, 1), half(hist_o, e, 1)
                key = e if e == "new" else (e, h)
                to_left = (here, right, kv_left)
                to_right = (here, left, kv_right)
                if prefill:
                    from_right[key] = Copy(FROM_RIGHT + n + h, [(here, right, direct), to_left if ring else None], (ring, ring))
                    from_left[key] = Copy(FROM_LEFT + n + h, [None, to_right if ring else None], (ring, ring))
                else:
                    from_right[key] = Copy(FROM_RIGHT + n + h, [None, to_left], (True, True))
                    from_left[key] = Copy(FROM_LEFT + n + h, [to_right, to_right], (True, True))
                    if e in (0, "new"):
                        t = h if e == 0 else 2
                        relays["right", key] = Copy(
                            FROM_RIGHT + n + h, [(right, right, partner), None], (False, False))
                        relays["left", key] = Copy(
                            FROM_LEFT + n + h, [(left, left, partner), None], (False, False), RELAY + t)
            ends = (low, to_low, kv_left)
            ends_high = (high, to_high, kv_right)
            if prefill:
                far_low[e] = Copy(FAR_LOW + f, [None, ends if ring else None], (ring, ring))
                far_high[e] = Copy(FAR_HIGH + f, [None, ends_high if ring else None], (ring, ring))
            else:
                far_low[e] = Copy(FAR_LOW + f, [ends, ends], (True, True))
                far_high[e] = Copy(FAR_HIGH + f, [ends_high, ends_high], (True, True))
                if e in (0, "new"):
                    t = RELAY + 3 + (2 if e == "new" else 0)
                    relays["low", e] = Copy(FAR_LOW + f, [(to_low, to_low, partner), None], (False, False), t)
                    relays["high", e] = Copy(FAR_HIGH + f, [(to_high, to_high, partner), None], (False, False), t + 1)
        late = [] if prefill else [1, 2, 3]
        pair = remote(PAIR, fresh_ref, fresh_all.at[0, me], partner)

        def tiles(slot, part):
            return q_all.at[pl.ds(slot * TILES + part * 2, 2)]

        own_query = [q_ref.at[pl.ds(0, 2)], q_ref.at[pl.ds(2, 2)]]
        queries = [
            remote(QUERY, own_query[0], tiles(1, 0), q_right),
            remote(QUERY + 1, own_query[1], tiles(2, 1), q_left),
            remote(QUERY + 2, own_query[1], tiles(1, 1), q_right),
            remote(QUERY + 3, own_query[0], tiles(2, 0), q_left),
            remote(QUERY + 4, tiles(1, 0), tiles(3, 0), q_right),
            remote(QUERY + 5, tiles(2, 1), tiles(3, 1), q_left),
        ]

        def hand_on(received, onward):
            received.wait_recv()
            onward.start()

        def decode_row(slot, tile):
            return row_block(slot) * (ROWS // STEPS) + tile * (TILE // STEPS)

        def tile_episode(slot, tile):
            return 0 if prefill else episode_ref[decode_row(slot, tile)]

        def compute(items, where, first=False):
            all_scores, all_values = [], []
            for i in items:
                slot, tile = i // TILES, i % TILES
                if i < MAIN:
                    query, episode = q_all[i], tile_episode(slot, tile)
                else:
                    query, episode = q_all[extra_tile[i - MAIN]], i - MAIN + 1
                parts, values = [], []
                for b in where:
                    if b == "new":
                        if prefill:
                            limit = row_block(slot) * ROWS + tile * TILE + lane_position
                        else:
                            limit = jnp.where(episode == 0, 2 * STRETCH, -1)
                        s = scores(fresh_all[:, :, :, 0:DIM].reshape(RING * 2 * NEW, DIM), query)
                        kept = []
                        for part in range(2 * RING):
                            base = part % 2 * STRETCH + blocks[part // 2] * NEW
                            kept.append(jnp.where(new_row <= limit - base, s[part * NEW:(part + 1) * NEW], MASKED))
                        parts.append(jnp.concatenate(kept, axis=0))
                        values.append(fresh_all[:, :, :, DIM:2 * DIM].reshape(RING * 2 * NEW, DIM))
                    else:
                        allowed = slot_row < len_ref[episode] - blocks[b] * SLOTS
                        parts.append(jnp.where(allowed, scores(buffers[b][episode, :, 0:DIM], query), MASKED))
                        values.append(buffers[b][episode, :, DIM:2 * DIM])
                all_scores.append(parts)
                all_values.append(values)
            update(items, all_scores, all_values, first)

        def state(slot, tile):
            i = slot * TILES + tile
            top, total, summed = acc_s[i, 0:1], acc_s[i, 1:2], acc_o[i]
            if prefill:
                return top, total, summed
            first = tile_episode(slot, tile)
            row_episode = jnp.zeros((1, LANES), jnp.int32)
            for r in range(TILE // STEPS):
                row_episode = jnp.where(
                    lane_position // STEPS == r, episode_ref[decode_row(slot, tile) + r], row_episode
                )
            for j in range(EXTRA):
                other = (row_episode == j + 1) & (first != j + 1)
                top = jnp.where(other, acc_s[MAIN + j, 0:1], top)
                total = jnp.where(other, acc_s[MAIN + j, 1:2], total)
                summed = jnp.where(other, acc_o[MAIN + j], summed)
            return top, total, summed

        def result(number, slot, part, into_o, into_s, device):
            n = (slot - 1) * 2 + part
            return (
                remote(RESULT + 2 * number, tx_o.at[n], into_o, device),
                remote(RESULT + 2 * number + 1, tx_s.at[n], into_s, device),
            )

        results = [
            result(0, 3, 0, mid_o.at[0], mid_s.at[0], q_right),
            result(1, 3, 1, mid_o.at[1], mid_s.at[1], q_left),
            result(2, 2, 1, fin_o.at[0, 1], fin_s.at[0, 1], q_right),
            result(3, 1, 0, fin_o.at[1, 0], fin_s.at[1, 0], q_left),
            result(4, 2, 0, fin_o.at[0, 0], fin_s.at[0, 0], q_right),
            result(5, 1, 1, fin_o.at[1, 1], fin_s.at[1, 1], q_left),
        ]

        def pack(slot, part, incoming=None):
            n = (slot - 1) * 2 + part
            for t in range(2):
                now = state(slot, part * 2 + t)
                if incoming is not None:
                    now = merge(now, load(mid_o.at[incoming], mid_s.at[incoming], t))
                tx_s[n, 2 * t:2 * t + 1] = now[0]
                tx_s[n, 2 * t + 1:2 * t + 2] = now[1]
                tx_o[n, t] = now[2].astype(jnp.bfloat16)

        def ship(number):
            for copy in results[number]:
                copy.start()

        def arrive(number):
            for copy in results[number]:
                copy.wait_recv()

        tx_s[...] = jnp.zeros_like(tx_s)
        pair.start()
        for h in range(2):
            from_right[0, h].start()
            from_left[0, 1 - h].start()
        for copy in queries[:4]:
            copy.start()
        if not prefill:
            for j in range(EXTRA):
                extra_tile[j] = 0
            for slot in range(RING):
                for tile in range(TILES):
                    low = tile_episode(slot, tile)
                    high = episode_ref[decode_row(slot, tile) + TILE // STEPS - 1]
                    for j in range(EXTRA):
                        hit = (low < j + 1) & (high >= j + 1)
                        extra_tile[j] = jnp.where(hit, slot * TILES + tile, extra_tile[j])
        compute(span(0, 4), [0], True)
        pair.wait_recv()
        from_right["new"].start()
        from_left["new"].start()
        for h in range(2):
            for e in (1, 2, 3):
                from_right[e, h].start()
                if not prefill:
                    from_left[e, 1 - h].start()
        hand_on(queries[0], queries[4])
        hand_on(queries[1], queries[5])

        def pass_on(side, key, *onward):
            {"right": from_right, "left": from_left, "low": far_low, "high": far_high}[side][key].wait_recv()
            if (side, key) in relays:
                relays[side, key].start()
            for copy in onward:
                copy.start()

        pass_on("right", (0, 0), far_low[0])
        pass_on("left", (0, 1), far_high[0])
        pass_on("right", (0, 1))
        pass_on("left", (0, 0))
        pass_on("right", "new", far_low["new"])
        pass_on("left", "new", far_high["new"])
        queries[2].wait_recv()
        queries[3].wait_recv()
        compute(span(4, 12), [0], True)
        if prefill:
            compute(span(0, 4), [1, 2])
            queries[4].wait_recv()
            queries[5].wait_recv()
            compute(span(12, 16), [0], True)
            compute(span(4, 8), [1, 2])
            compute(span(8, 12), [1, 2])
            compute(span(12, 16), [1, 2])
            for e in (0, "new"):
                far_low[e].wait_recv()
                far_high[e].wait_recv()
            last = ["new", 3]
            compute(span(12, 16), last)
        else:
            pass_on("right", (1, 0), far_low[1])
            pass_on("left", (1, 1), far_high[1])
            queries[4].wait_recv()
            queries[5].wait_recv()
            for e in (0, "new"):
                pass_on("low", e)
                pass_on("high", e)
            compute(span(12, 19), [0], True)
            pass_on("right", (2, 0), far_low[2])
            pass_on("left", (2, 1), far_high[2])
            compute(span(0, 4), ["new"])
            compute(span(4, 8), ["new"])
            pass_on("right", (3, 0), far_low[3])
            pass_on("left", (3, 1), far_high[3])
            compute(span(8, 12), ["new"])
            compute(span(12, 16), ["new"])
            for e in late:
                from_right[e, 1].wait_recv()
            compute(span(0, 8), [1])
            compute(span(8, 19), [1])
            for e in late:
                from_left[e, 0].wait_recv()
            compute(span(0, 8), [2])
            compute(span(8, 19), [2])
            for e in late:
                far_low[e].wait_recv()
                far_high[e].wait_recv()
            last = [3]
            compute(span(12, 19), last)
        pack(3, 0)
        ship(0)
        pack(3, 1)
        ship(1)
        compute(span(4, 12), last)
        pack(2, 1)
        ship(2)
        pack(1, 0)
        ship(3)
        arrive(0)
        pack(2, 0, 0)
        ship(4)
        arrive(1)
        pack(1, 1, 1)
        ship(5)
        compute(span(0, 4), last)

        for number in (2, 3, 4, 5):
            arrive(number)
        for tile in range(TILES):
            now = state(0, tile)
            for side in range(2):
                now = merge(now, load(fin_o.at[side, tile // 2], fin_s.at[side, tile // 2], tile % 2))
            whole = (now[2] * (1.0 / now[1])).T.astype(jnp.bfloat16)
            for h in range(HEADS):
                out_ref[tile, :, h * DIM:(h + 1) * DIM] = whole[h * TILE:(h + 1) * TILE]

        sent = [pair] + queries + [c for both in results for c in both]
        for table in (from_right, from_left, far_low, far_high, relays):
            sent += list(table.values())
        for copy in sent:
            copy.wait_send()

    @pl.when(grp == 0)
    def _():
        program(True)

    @pl.when(grp == 1)
    def _():
        program(False)


def local(queries, history_cache, fresh_cache, hist_len, decode_episode):
    vmem = pl.BlockSpec(memory_space=pltpu.VMEM)
    bf16, f32 = jnp.bfloat16, jnp.float32
    block = pltpu.VMEM((EPISODES, SLOTS, 2 * DIM), bf16)
    out = pl.pallas_call(
        kernel,
        out_shape=jax.ShapeDtypeStruct((TILES, TILE, HEADS * DIM), bf16),
        in_specs=[pl.BlockSpec(memory_space=pl.ANY)] * 5,
        out_specs=vmem,
        scratch_shapes=[
            pltpu.SMEM((EPISODES,), jnp.int32),
            pltpu.SMEM((512,), jnp.int32),
            block,
            block,
            block,
            block,
            pltpu.VMEM((RING, 2, NEW, 2 * DIM), bf16),
            pltpu.VMEM((MAIN, TILE, HEADS * DIM), bf16),
            pltpu.VMEM((MAIN + EXTRA, DIM, LANES), f32),
            pltpu.VMEM((MAIN + EXTRA, 8, LANES), f32),
            pltpu.VMEM((6, 2, DIM, LANES), bf16),
            pltpu.VMEM((6, 8, LANES), f32),
            pltpu.VMEM((2, 2, DIM, LANES), bf16),
            pltpu.VMEM((2, 8, LANES), f32),
            pltpu.VMEM((2, 2, 2, DIM, LANES), bf16),
            pltpu.VMEM((2, 2, 8, LANES), f32),
            pltpu.SMEM((EXTRA,), jnp.int32),
            pltpu.SemaphoreType.DMA((COPIES,)),
            pltpu.SemaphoreType.DMA((COPIES,)),
            pltpu.SemaphoreType.DMA((5,)),
        ],
        compiler_params=pltpu.CompilerParams(
            collective_id=0, has_side_effects=True, vmem_limit_bytes=56 * 1024 * 1024
        ),
    )(
        queries.reshape(TILES, TILE, HEADS * DIM),
        history_cache.reshape(EPISODES, SLOTS, 2 * DIM),
        fresh_cache.reshape(NEW, 2 * DIM),
        hist_len,
        decode_episode,
    )
    return out.reshape(1, ROWS, HEADS * DIM)


def solution(mesh):
    placed = (
        P("grp", "ctx", "head"),
        P(None, "ctx", "head", None),
        P("grp", "ctx", "head", None),
        P(),
        P(),
    )
    return jax.shard_map(
        local, mesh=mesh, in_specs=placed, out_specs=P("grp", "ctx", "head"), check_vma=False
    )
```

```python
import functools
import math

import jax
import jax.numpy as jnp
from jax import lax
from jax.experimental import pallas as pl
from jax.experimental.pallas import tpu as pltpu
from jax.sharding import PartitionSpec as P

MESH = pl.DeviceIdType.MESH
STEPS = 4
RING = 4
EPISODES = 4
HEADS = 8
DIM = 128
SLOTS = 256
HALF = 128
NEW = 64
TILE = 32
LANES = TILE * HEADS
ROWS = 128
TILES = ROWS // TILE
MAIN = RING * TILES
EXTRA = EPISODES - 1
STRETCH = 1024
MASKED = -1e30
SCALE = math.log2(math.e) / math.sqrt(DIM)

FROM_RIGHT, FROM_LEFT, FAR_LOW, FAR_HIGH, PAIR, QUERY, RESULT = 0, 9, 18, 23, 28, 29, 35
RELAY = 47
COPIES = 54


def kernel(
    q_ref, hist_ref, fresh_ref, len_in, episode_in, out_ref,
    len_ref, episode_ref, hist_own, hist_d, hist_y, hist_o, fresh_all, q_all,
    acc_o, acc_s, tx_o, tx_s, mid_o, mid_s, fin_o, fin_s, extra_tile,
    send, recv, inside,
):
    ctx = lax.axis_index("ctx")
    grp = lax.axis_index("grp")
    core = lax.axis_index("head") % 2
    x, k = ctx // RING, ctx % RING
    buffers = (hist_own, hist_d, hist_y, hist_o)

    def place(x_at, k_at):
        return (x_at + RING) % RING * RING + (k_at + RING) % RING

    direct = {"ctx": place(x, k + 2 * grp - 1), "grp": 1 - grp}
    partner = {"ctx": ctx, "grp": 1 - grp}
    x_right, x_left = {"ctx": place(x + 1, k)}, {"ctx": place(x - 1, k)}
    z_right, z_left = {"ctx": place(x, k + 1)}, {"ctx": place(x, k - 1)}

    def remote(number, src, dst, device, sender=None):
        return pltpu.make_async_remote_copy(
            src_ref=src, dst_ref=dst, send_sem=send.at[number if sender is None else sender], recv_sem=recv.at[number],
            device_id=device, device_id_type=MESH,
        )

    local_copies = [
        pltpu.make_async_copy(src, dst, inside.at[n])
        for n, (src, dst) in enumerate([
            (len_in, len_ref), (episode_in, episode_ref), (fresh_ref, fresh_all.at[0, grp]),
            (q_ref, q_all.at[pl.ds(0, TILES)]), (hist_ref, hist_own),
        ])
    ]
    for copy in local_copies:
        copy.start()

    barrier = pltpu.get_barrier_semaphore()

    def greet(device):
        pl.semaphore_signal(barrier, inc=1, device_id=device, device_id_type=MESH)

    greet(partner)
    greet(x_right)
    greet(x_left)

    @pl.when(core == 0)
    def _():
        greet(direct)

    @pl.when(core + grp > 0)
    def _():
        greet(z_right)
        greet(z_left)

    pl.semaphore_wait(barrier, jnp.where(core == 1, 5, 4 + 2 * grp))
    for copy in local_copies:
        copy.wait()

    lane = lax.broadcasted_iota(jnp.int32, (1, LANES), 1)
    lane_position = lane % TILE
    slot_row = lax.broadcasted_iota(jnp.int32, (SLOTS, LANES), 0)
    new_row = lax.broadcasted_iota(jnp.int32, (NEW, LANES), 0)

    def half(ref, episode, which):
        if not isinstance(which, int):
            which = pl.multiple_of(which * HALF, HALF)
        else:
            which = which * HALF
        return ref.at[episode, pl.ds(which, HALF)]

    def stack_heads(block):
        return jnp.concatenate([block[:, h * DIM:(h + 1) * DIM] for h in range(HEADS)], axis=0)

    def scores(keys, block):
        return lax.dot_general(keys, stack_heads(block), (((1,), (1,)), ((), ())), preferred_element_type=jnp.float32)

    def update(items, all_scores, all_values, first):
        tops = []
        for parts in all_scores:
            top = jnp.max(parts[0], axis=0, keepdims=True)
            for s in parts[1:]:
                top = jnp.maximum(top, jnp.max(s, axis=0, keepdims=True))
            tops.append(top)
        if not first:
            olds = [(acc_s[i, 0:1], acc_s[i, 1:2]) for i in items]
            tops = [jnp.maximum(top, old[0]) for top, old in zip(tops, olds)]
        weights = [[jnp.exp2(s * SCALE - top * SCALE) for s in parts] for parts, top in zip(all_scores, tops)]
        totals = [sum(jnp.sum(p, axis=0, keepdims=True) for p in parts) for parts in weights]
        sums = [
            sum(
                lax.dot_general(v, p.astype(jnp.bfloat16), (((0,), (0,)), ((), ())), preferred_element_type=jnp.float32)
                for v, p in zip(values, parts)
            )
            for values, parts in zip(all_values, weights)
        ]
        if not first:
            rescales = [jnp.exp2((old[0] - top) * SCALE) for old, top in zip(olds, tops)]
            totals = [total + old[1] * r for total, old, r in zip(totals, olds, rescales)]
            sums = [summed + acc_o[i] * r for i, summed, r in zip(items, sums, rescales)]
        for i, top, total, summed in zip(items, tops, totals, sums):
            acc_s[i, 0:1] = top
            acc_s[i, 1:2] = total
            acc_o[i] = summed

    def merge(one, two):
        top = jnp.maximum(one[0], two[0])
        a, b = jnp.exp2((one[0] - top) * SCALE), jnp.exp2((two[0] - top) * SCALE)
        return top, one[1] * a + two[1] * b, one[2] * a + two[2] * b

    def load(o_ref, s_ref, tile):
        return s_ref[2 * tile:2 * tile + 1], s_ref[2 * tile + 1:2 * tile + 2], o_ref[tile].astype(jnp.float32)

    def span(first, last):
        return list(range(first, last))

    class Copy:
        def __init__(self, number, ends, receives, sender=None):
            self.number, self.ends, self.receives, self.sender = number, ends, receives, sender

        def each(self, wanted, act):
            if all(wanted) and self.ends[0] is self.ends[1]:
                act(0)
                return
            for c in range(2):
                if wanted[c]:
                    pl.when(core == c)(functools.partial(act, c))

        def of(self, ends):
            return remote(self.number, *ends, self.sender)

        def start(self):
            self.each([e is not None for e in self.ends], lambda c: self.of(self.ends[c]).start())

        def wait_send(self):
            self.each([e is not None for e in self.ends], lambda c: self.of(self.ends[c]).wait_send())

        def wait_recv(self):
            ends = self.ends[0] or self.ends[1]
            if all(self.receives):
                self.of(ends).wait_recv()
            else:
                self.each(self.receives, lambda c: self.of(ends).wait_recv())

    def program(prefill):
        me = 0 if prefill else 1
        def either(one, two):
            return {"ctx": jnp.where(core == 1, one["ctx"], two["ctx"])}

        if prefill:
            kv_right, kv_left, q_right, q_left = z_right, z_left, x_right, x_left
            blocks = [place(x, k + off) for off in (0, 1, -1, 2)]
        else:
            kv_right, kv_left = either(x_right, z_right), either(x_left, z_left)
            q_right, q_left = either(z_right, x_right), either(z_left, x_left)
            blocks = [jnp.where(core == 1, place(x + off, k), place(x, k + off)) for off in (0, 1, -1, 2)]

        def row_block(slot):
            off = (0, -1, 1, 2)[slot]
            if prefill:
                return place(x + off, k)
            return jnp.where(core == 1, place(x, k + off), place(x + off, k))

        from_right, from_left, far_low, far_high, relays = {}, {}, {}, {}, {}
        for e in list(range(EPISODES)) + ["new"]:
            ring = not prefill or e in (0, "new")
            n = 2 * EPISODES if e == "new" else 2 * e
            f = EPISODES if e == "new" else e
            for h in range(2 if e != "new" else 1):
                if e == "new":
                    here, right, left = fresh_all.at[0], fresh_all.at[1], fresh_all.at[2]
                    low, to_low = fresh_all.at[1, 0], fresh_all.at[3, 0]
                    high, to_high = fresh_all.at[2, 1], fresh_all.at[3, 1]
                else:
                    here, right, left = half(hist_ref, e, h), half(hist_d, e, h), half(hist_y, e, h)
                    low, to_low = half(hist_d, e, 0), half(hist_o, e, 0)
                    high, to_high = half(hist_y, e, 1), half(hist_o, e, 1)
                key = e if e == "new" else (e, h)
                to_left = (here, right, kv_left)
                to_right = (here, left, kv_right)
                if prefill:
                    from_right[key] = Copy(FROM_RIGHT + n + h, [(here, right, direct), to_left if ring else None], (ring, ring))
                    from_left[key] = Copy(FROM_LEFT + n + h, [None, to_right if ring else None], (ring, ring))
                else:
                    from_right[key] = Copy(FROM_RIGHT + n + h, [None, to_left], (True, True))
                    from_left[key] = Copy(FROM_LEFT + n + h, [to_right, to_right], (True, True))
                    if e in (0, "new"):
                        t = h if e == 0 else 2
                        relays["right", key] = Copy(
                            FROM_RIGHT + n + h, [(right, right, partner), None], (False, False))
                        relays["left", key] = Copy(
                            FROM_LEFT + n + h, [(left, left, partner), None], (False, False), RELAY + t)
            ends = (low, to_low, kv_left)
            ends_high = (high, to_high, kv_right)
            if prefill:
                far_low[e] = Copy(FAR_LOW + f, [None, ends if ring else None], (ring, ring))
                far_high[e] = Copy(FAR_HIGH + f, [None, ends_high if ring else None], (ring, ring))
            else:
                far_low[e] = Copy(FAR_LOW + f, [ends, ends], (True, True))
                far_high[e] = Copy(FAR_HIGH + f, [ends_high, ends_high], (True, True))
                if e in (0, "new"):
                    t = RELAY + 3 + (2 if e == "new" else 0)
                    relays["low", e] = Copy(FAR_LOW + f, [(to_low, to_low, partner), None], (False, False), t)
                    relays["high", e] = Copy(FAR_HIGH + f, [(to_high, to_high, partner), None], (False, False), t + 1)
        late = [] if prefill else [1, 2, 3]
        pair = remote(PAIR, fresh_ref, fresh_all.at[0, me], partner)

        def tiles(slot, part):
            return q_all.at[pl.ds(slot * TILES + part * 2, 2)]

        own_query = [q_ref.at[pl.ds(0, 2)], q_ref.at[pl.ds(2, 2)]]
        queries = [
            remote(QUERY, own_query[0], tiles(1, 0), q_right),
            remote(QUERY + 1, own_query[1], tiles(2, 1), q_left),
            remote(QUERY + 2, own_query[1], tiles(1, 1), q_right),
            remote(QUERY + 3, own_query[0], tiles(2, 0), q_left),
            remote(QUERY + 4, tiles(1, 0), tiles(3, 0), q_right),
            remote(QUERY + 5, tiles(2, 1), tiles(3, 1), q_left),
        ]

        def hand_on(received, onward):
            received.wait_recv()
            onward.start()

        def decode_row(slot, tile):
            return row_block(slot) * (ROWS // STEPS) + tile * (TILE // STEPS)

        def tile_episode(slot, tile):
            return 0 if prefill else episode_ref[decode_row(slot, tile)]

        def compute(items, where, first=False):
            all_scores, all_values = [], []
            for i in items:
                slot, tile = i // TILES, i % TILES
                if i < MAIN:
                    query, episode = q_all[i], tile_episode(slot, tile)
                else:
                    query, episode = q_all[extra_tile[i - MAIN]], i - MAIN + 1
                parts, values = [], []
                for b in where:
                    if b == "new":
                        if prefill:
                            limit = row_block(slot) * ROWS + tile * TILE + lane_position
                        else:
                            limit = jnp.where(episode == 0, 2 * STRETCH, -1)
                        s = scores(fresh_all[:, :, :, 0:DIM].reshape(RING * 2 * NEW, DIM), query)
                        kept = []
                        for part in range(2 * RING):
                            base = part % 2 * STRETCH + blocks[part // 2] * NEW
                            kept.append(jnp.where(new_row <= limit - base, s[part * NEW:(part + 1) * NEW], MASKED))
                        parts.append(jnp.concatenate(kept, axis=0))
                        values.append(fresh_all[:, :, :, DIM:2 * DIM].reshape(RING * 2 * NEW, DIM))
                    elif isinstance(b, str):
                        t = 0 if b == "new0" else 1
                        limit = row_block(slot) * ROWS + tile * TILE + lane_position
                        s = scores(fresh_all[:, t, :, 0:DIM].reshape(RING * NEW, DIM), query)
                        kept = []
                        for part in range(RING):
                            base = t * STRETCH + blocks[part] * NEW
                            kept.append(jnp.where(new_row <= limit - base, s[part * NEW:(part + 1) * NEW], MASKED))
                        parts.append(jnp.concatenate(kept, axis=0))
                        values.append(fresh_all[:, t, :, DIM:2 * DIM].reshape(RING * NEW, DIM))
                    else:
                        allowed = slot_row < len_ref[episode] - blocks[b] * SLOTS
                        parts.append(jnp.where(allowed, scores(buffers[b][episode, :, 0:DIM], query), MASKED))
                        values.append(buffers[b][episode, :, DIM:2 * DIM])
                all_scores.append(parts)
                all_values.append(values)
            update(items, all_scores, all_values, first)

        def state(slot, tile):
            i = slot * TILES + tile
            top, total, summed = acc_s[i, 0:1], acc_s[i, 1:2], acc_o[i]
            if prefill:
                return top, total, summed
            first = tile_episode(slot, tile)
            row_episode = jnp.zeros((1, LANES), jnp.int32)
            for r in range(TILE // STEPS):
                row_episode = jnp.where(
                    lane_position // STEPS == r, episode_ref[decode_row(slot, tile) + r], row_episode
                )
            for j in range(EXTRA):
                other = (row_episode == j + 1) & (first != j + 1)
                top = jnp.where(other, acc_s[MAIN + j, 0:1], top)
                total = jnp.where(other, acc_s[MAIN + j, 1:2], total)
                summed = jnp.where(other, acc_o[MAIN + j], summed)
            return top, total, summed

        def result(number, slot, part, into_o, into_s, device):
            n = (slot - 1) * 2 + part
            return (
                remote(RESULT + 2 * number, tx_o.at[n], into_o, device),
                remote(RESULT + 2 * number + 1, tx_s.at[n], into_s, device),
            )

        results = [
            result(0, 3, 0, mid_o.at[0], mid_s.at[0], q_right),
            result(1, 3, 1, mid_o.at[1], mid_s.at[1], q_left),
            result(2, 2, 1, fin_o.at[0, 1], fin_s.at[0, 1], q_right),
            result(3, 1, 0, fin_o.at[1, 0], fin_s.at[1, 0], q_left),
            result(4, 2, 0, fin_o.at[0, 0], fin_s.at[0, 0], q_right),
            result(5, 1, 1, fin_o.at[1, 1], fin_s.at[1, 1], q_left),
        ]

        def pack(slot, part, incoming=None):
            n = (slot - 1) * 2 + part
            for t in range(2):
                now = state(slot, part * 2 + t)
                if incoming is not None:
                    now = merge(now, load(mid_o.at[incoming], mid_s.at[incoming], t))
                tx_s[n, 2 * t:2 * t + 1] = now[0]
                tx_s[n, 2 * t + 1:2 * t + 2] = now[1]
                tx_o[n, t] = now[2].astype(jnp.bfloat16)

        def ship(number):
            for copy in results[number]:
                copy.start()

        def arrive(number):
            for copy in results[number]:
                copy.wait_recv()

        tx_s[...] = jnp.zeros_like(tx_s)
        pair.start()
        for h in range(2):
            from_right[0, h].start()
            from_left[0, 1 - h].start()
        for copy in queries[:4]:
            copy.start()
        if not prefill:
            for j in range(EXTRA):
                extra_tile[j] = 0
            for slot in range(RING):
                for tile in range(TILES):
                    low = tile_episode(slot, tile)
                    high = episode_ref[decode_row(slot, tile) + TILE // STEPS - 1]
                    for j in range(EXTRA):
                        hit = (low < j + 1) & (high >= j + 1)
                        extra_tile[j] = jnp.where(hit, slot * TILES + tile, extra_tile[j])
        compute(span(0, 4), [0], True)
        pair.wait_recv()
        from_right["new"].start()
        from_left["new"].start()

        def send(h, *episodes):
            for e in episodes:
                from_right[e, h].start()
                if not prefill:
                    from_left[e, 1 - h].start()

        def pass_on(side, key, *onward):
            {"right": from_right, "left": from_left, "low": far_low, "high": far_high}[side][key].wait_recv()
            if (side, key) in relays:
                relays[side, key].start()
            for copy in onward:
                copy.start()

        send(0, 1, 2, 3)
        if prefill:
            send(1, 1, 2, 3)
        hand_on(queries[0], queries[4])
        hand_on(queries[1], queries[5])
        pass_on("right", (0, 0), far_low[0])
        pass_on("left", (0, 1), far_high[0])
        if not prefill:
            send(1, 1)
        pass_on("right", (0, 1))
        pass_on("left", (0, 0))
        pass_on("right", "new", far_low["new"])
        pass_on("left", "new", far_high["new"])
        if not prefill:
            send(1, 2, 3)
        queries[2].wait_recv()
        queries[3].wait_recv()
        compute(span(4, 12), [0], True)
        if prefill:
            compute(span(0, 4), [1, 2])
            compute(span(4, 8), [1, 2])
            compute(span(8, 12), [1, 2])
            queries[4].wait_recv()
            queries[5].wait_recv()
            compute(span(12, 16), [0, 1, 2], True)
            for e in (0, "new"):
                far_low[e].wait_recv()
                far_high[e].wait_recv()
            last = ["new0", 3]

            def second(*slots):
                for slot in slots:
                    pl.when(row_block(slot) * ROWS >= STRETCH)(
                        functools.partial(compute, span(slot * TILES, slot * TILES + TILES), ["new1"]))

            compute(span(12, 16), last)
            second(3)
        else:
            for e in late:
                pass_on("right", (e, 0), far_low[e])
                pass_on("left", (e, 1), far_high[e])
            pass_on("low", 0)
            pass_on("high", 0)
            queries[4].wait_recv()
            queries[5].wait_recv()
            compute(span(12, 19), [0], True)
            pass_on("low", "new")
            pass_on("high", "new")
            compute(span(0, 4), ["new"])
            for slot in range(1, RING):
                compute(span(slot * TILES, slot * TILES + TILES), ["new"])
            for e in late:
                from_right[e, 1].wait_recv()
                from_left[e, 0].wait_recv()
            compute(span(0, 5), [1, 2])
            compute(span(5, 10), [1, 2])
            compute(span(10, 15), [1, 2])
            compute(span(15, 19), [1, 2])
            for e in late:
                far_low[e].wait_recv()
                far_high[e].wait_recv()
            last = [3]
            compute(span(12, 19), last)
        pack(3, 0)
        ship(0)
        pack(3, 1)
        ship(1)
        if prefill:
            compute(span(8, 12), last)
            second(2)
            pack(2, 1)
            ship(2)
            compute(span(4, 8), last)
            second(1)
        else:
            compute(span(4, 12), last)
            pack(2, 1)
            ship(2)
        pack(1, 0)
        ship(3)
        arrive(0)
        pack(2, 0, 0)
        ship(4)
        arrive(1)
        pack(1, 1, 1)
        ship(5)
        compute(span(0, 4), last)
        if prefill:
            second(0)

        for number in (2, 3, 4, 5):
            arrive(number)
        for tile in range(TILES):
            now = state(0, tile)
            for side in range(2):
                now = merge(now, load(fin_o.at[side, tile // 2], fin_s.at[side, tile // 2], tile % 2))
            whole = (now[2] * (1.0 / now[1])).T.astype(jnp.bfloat16)
            for h in range(HEADS):
                out_ref[tile, :, h * DIM:(h + 1) * DIM] = whole[h * TILE:(h + 1) * TILE]

        sent = [pair] + queries + [c for both in results for c in both]
        for table in (from_right, from_left, far_low, far_high, relays):
            sent += list(table.values())
        for copy in sent:
            copy.wait_send()

    @pl.when(grp == 0)
    def _():
        program(True)

    @pl.when(grp == 1)
    def _():
        program(False)


def local(queries, history_cache, fresh_cache, hist_len, decode_episode):
    vmem = pl.BlockSpec(memory_space=pltpu.VMEM)
    bf16, f32 = jnp.bfloat16, jnp.float32
    block = pltpu.VMEM((EPISODES, SLOTS, 2 * DIM), bf16)
    out = pl.pallas_call(
        kernel,
        out_shape=jax.ShapeDtypeStruct((TILES, TILE, HEADS * DIM), bf16),
        in_specs=[pl.BlockSpec(memory_space=pl.ANY)] * 5,
        out_specs=vmem,
        scratch_shapes=[
            pltpu.SMEM((EPISODES,), jnp.int32),
            pltpu.SMEM((512,), jnp.int32),
            block,
            block,
            block,
            block,
            pltpu.VMEM((RING, 2, NEW, 2 * DIM), bf16),
            pltpu.VMEM((MAIN, TILE, HEADS * DIM), bf16),
            pltpu.VMEM((MAIN + EXTRA, DIM, LANES), f32),
            pltpu.VMEM((MAIN + EXTRA, 8, LANES), f32),
            pltpu.VMEM((6, 2, DIM, LANES), bf16),
            pltpu.VMEM((6, 8, LANES), f32),
            pltpu.VMEM((2, 2, DIM, LANES), bf16),
            pltpu.VMEM((2, 8, LANES), f32),
            pltpu.VMEM((2, 2, 2, DIM, LANES), bf16),
            pltpu.VMEM((2, 2, 8, LANES), f32),
            pltpu.SMEM((EXTRA,), jnp.int32),
            pltpu.SemaphoreType.DMA((COPIES,)),
            pltpu.SemaphoreType.DMA((COPIES,)),
            pltpu.SemaphoreType.DMA((5,)),
        ],
        compiler_params=pltpu.CompilerParams(
            collective_id=0, has_side_effects=True, vmem_limit_bytes=56 * 1024 * 1024
        ),
    )(
        queries.reshape(TILES, TILE, HEADS * DIM),
        history_cache.reshape(EPISODES, SLOTS, 2 * DIM),
        fresh_cache.reshape(NEW, 2 * DIM),
        hist_len,
        decode_episode,
    )
    return out.reshape(1, ROWS, HEADS * DIM)


def solution(mesh):
    placed = (
        P("grp", "ctx", "head"),
        P(None, "ctx", "head", None),
        P("grp", "ctx", "head", None),
        P(),
        P(),
    )
    return jax.shard_map(
        local, mesh=mesh, in_specs=placed, out_specs=P("grp", "ctx", "head"), check_vma=False
    )
```

```python
import functools
import math

import jax
import jax.numpy as jnp
from jax import lax
from jax.experimental import pallas as pl
from jax.experimental.pallas import tpu as pltpu
from jax.sharding import PartitionSpec as P

MESH = pl.DeviceIdType.MESH
STEPS = 4
RING = 4
EPISODES = 4
HEADS = 8
DIM = 128
SLOTS = 256
HALF = 128
NEW = 64
TILE = 32
LANES = TILE * HEADS
ROWS = 128
TILES = ROWS // TILE
MAIN = RING * TILES
EXTRA = EPISODES - 1
STRETCH = 1024
MASKED = -1e30
SCALE = math.log2(math.e) / math.sqrt(DIM)

FROM_RIGHT, FROM_LEFT, FAR_LOW, FAR_HIGH, PAIR, QUERY, RESULT = 0, 9, 18, 23, 28, 29, 35
RELAY = 47
COPIES = 54


def kernel(
    q_ref, hist_ref, fresh_ref, len_in, episode_in, out_ref,
    len_ref, episode_ref, hist_own, hist_d, hist_y, hist_o, fresh_all, q_all,
    acc_o, acc_s, tx_o, tx_s, mid_o, mid_s, fin_o, fin_s, extra_tile,
    send, recv, inside,
):
    ctx = lax.axis_index("ctx")
    grp = lax.axis_index("grp")
    core = lax.axis_index("head") % 2
    x, k = ctx // RING, ctx % RING
    buffers = (hist_own, hist_d, hist_y, hist_o)

    def place(x_at, k_at):
        return (x_at + RING) % RING * RING + (k_at + RING) % RING

    direct = {"ctx": place(x, k + 2 * grp - 1), "grp": 1 - grp}
    partner = {"ctx": ctx, "grp": 1 - grp}
    x_right, x_left = {"ctx": place(x + 1, k)}, {"ctx": place(x - 1, k)}
    z_right, z_left = {"ctx": place(x, k + 1)}, {"ctx": place(x, k - 1)}

    def remote(number, src, dst, device, sender=None):
        return pltpu.make_async_remote_copy(
            src_ref=src, dst_ref=dst, send_sem=send.at[number if sender is None else sender], recv_sem=recv.at[number],
            device_id=device, device_id_type=MESH,
        )

    barrier = pltpu.get_barrier_semaphore()

    def greet(device):
        pl.semaphore_signal(barrier, inc=1, device_id=device, device_id_type=MESH)

    greet(partner)
    greet(x_right)
    greet(x_left)

    @pl.when(core == 0)
    def _():
        greet(direct)

    @pl.when(core + grp > 0)
    def _():
        greet(z_right)
        greet(z_left)

    local_copies = [
        pltpu.make_async_copy(src, dst, inside.at[n])
        for n, (src, dst) in enumerate([
            (len_in, len_ref), (episode_in, episode_ref), (fresh_ref, fresh_all.at[0, grp]),
            (q_ref, q_all.at[pl.ds(0, TILES)]), (hist_ref, hist_own),
        ])
    ]
    for copy in local_copies:
        copy.start()

    pl.semaphore_wait(barrier, jnp.where(core == 1, 5, 4 + 2 * grp))

    lane = lax.broadcasted_iota(jnp.int32, (1, LANES), 1)
    lane_position = lane % TILE
    slot_row = lax.broadcasted_iota(jnp.int32, (SLOTS, LANES), 0)
    new_row = lax.broadcasted_iota(jnp.int32, (NEW, LANES), 0)

    def half(ref, episode, which):
        if not isinstance(which, int):
            which = pl.multiple_of(which * HALF, HALF)
        else:
            which = which * HALF
        return ref.at[episode, pl.ds(which, HALF)]

    def stack_heads(block):
        return jnp.concatenate([block[:, h * DIM:(h + 1) * DIM] for h in range(HEADS)], axis=0)

    def scores(keys, block):
        return lax.dot_general(keys, stack_heads(block), (((1,), (1,)), ((), ())), preferred_element_type=jnp.float32)

    def update(items, all_scores, all_values, first):
        tops = []
        for parts in all_scores:
            top = jnp.max(parts[0], axis=0, keepdims=True)
            for s in parts[1:]:
                top = jnp.maximum(top, jnp.max(s, axis=0, keepdims=True))
            tops.append(top)
        if not first:
            olds = [(acc_s[i, 0:1], acc_s[i, 1:2]) for i in items]
            tops = [jnp.maximum(top, old[0]) for top, old in zip(tops, olds)]
        weights = [[jnp.exp2(s * SCALE - top * SCALE) for s in parts] for parts, top in zip(all_scores, tops)]
        totals = [sum(jnp.sum(p, axis=0, keepdims=True) for p in parts) for parts in weights]
        sums = [
            sum(
                lax.dot_general(v, p.astype(jnp.bfloat16), (((0,), (0,)), ((), ())), preferred_element_type=jnp.float32)
                for v, p in zip(values, parts)
            )
            for values, parts in zip(all_values, weights)
        ]
        if not first:
            rescales = [jnp.exp2((old[0] - top) * SCALE) for old, top in zip(olds, tops)]
            totals = [total + old[1] * r for total, old, r in zip(totals, olds, rescales)]
            sums = [summed + acc_o[i] * r for i, summed, r in zip(items, sums, rescales)]
        for i, top, total, summed in zip(items, tops, totals, sums):
            acc_s[i, 0:1] = top
            acc_s[i, 1:2] = total
            acc_o[i] = summed

    def merge(one, two):
        top = jnp.maximum(one[0], two[0])
        a, b = jnp.exp2((one[0] - top) * SCALE), jnp.exp2((two[0] - top) * SCALE)
        return top, one[1] * a + two[1] * b, one[2] * a + two[2] * b

    def load(o_ref, s_ref, tile):
        return s_ref[2 * tile:2 * tile + 1], s_ref[2 * tile + 1:2 * tile + 2], o_ref[tile].astype(jnp.float32)

    def span(first, last):
        return list(range(first, last))

    class Copy:
        def __init__(self, number, ends, receives, sender=None):
            self.number, self.ends, self.receives, self.sender = number, ends, receives, sender

        def each(self, wanted, act):
            if all(wanted) and self.ends[0] is self.ends[1]:
                act(0)
                return
            for c in range(2):
                if wanted[c]:
                    pl.when(core == c)(functools.partial(act, c))

        def of(self, ends):
            return remote(self.number, *ends, self.sender)

        def start(self):
            self.each([e is not None for e in self.ends], lambda c: self.of(self.ends[c]).start())

        def wait_send(self):
            self.each([e is not None for e in self.ends], lambda c: self.of(self.ends[c]).wait_send())

        def wait_recv(self):
            ends = self.ends[0] or self.ends[1]
            if all(self.receives):
                self.of(ends).wait_recv()
            else:
                self.each(self.receives, lambda c: self.of(ends).wait_recv())

    def program(prefill):
        me = 0 if prefill else 1
        def either(one, two):
            return {"ctx": jnp.where(core == 1, one["ctx"], two["ctx"])}

        if prefill:
            kv_right, kv_left, q_right, q_left = z_right, z_left, x_right, x_left
            blocks = [place(x, k + off) for off in (0, 1, -1, 2)]
        else:
            kv_right, kv_left = either(x_right, z_right), either(x_left, z_left)
            q_right, q_left = either(z_right, x_right), either(z_left, x_left)
            blocks = [jnp.where(core == 1, place(x + off, k), place(x, k + off)) for off in (0, 1, -1, 2)]

        def row_block(slot):
            off = (0, -1, 1, 2)[slot]
            if prefill:
                return place(x + off, k)
            return jnp.where(core == 1, place(x, k + off), place(x + off, k))

        from_right, from_left, far_low, far_high, relays = {}, {}, {}, {}, {}
        for e in list(range(EPISODES)) + ["new"]:
            ring = not prefill or e in (0, "new")
            n = 2 * EPISODES if e == "new" else 2 * e
            f = EPISODES if e == "new" else e
            for h in range(2 if e != "new" else 1):
                if e == "new":
                    here, right, left = fresh_all.at[0], fresh_all.at[1], fresh_all.at[2]
                    low, to_low = fresh_all.at[1, 0], fresh_all.at[3, 0]
                    high, to_high = fresh_all.at[2, 1], fresh_all.at[3, 1]
                else:
                    here, right, left = half(hist_ref, e, h), half(hist_d, e, h), half(hist_y, e, h)
                    low, to_low = half(hist_d, e, 0), half(hist_o, e, 0)
                    high, to_high = half(hist_y, e, 1), half(hist_o, e, 1)
                key = e if e == "new" else (e, h)
                to_left = (here, right, kv_left)
                to_right = (here, left, kv_right)
                if prefill:
                    from_right[key] = Copy(FROM_RIGHT + n + h, [(here, right, direct), to_left if ring else None], (ring, ring))
                    from_left[key] = Copy(FROM_LEFT + n + h, [None, to_right if ring else None], (ring, ring))
                else:
                    from_right[key] = Copy(FROM_RIGHT + n + h, [None, to_left], (True, True))
                    from_left[key] = Copy(FROM_LEFT + n + h, [to_right, to_right], (True, True))
                    if e in (0, "new"):
                        t = h if e == 0 else 2
                        relays["right", key] = Copy(
                            FROM_RIGHT + n + h, [(right, right, partner), None], (False, False))
                        relays["left", key] = Copy(
                            FROM_LEFT + n + h, [(left, left, partner), None], (False, False), RELAY + t)
            ends = (low, to_low, kv_left)
            ends_high = (high, to_high, kv_right)
            if prefill:
                far_low[e] = Copy(FAR_LOW + f, [None, ends if ring else None], (ring, ring))
                far_high[e] = Copy(FAR_HIGH + f, [None, ends_high if ring else None], (ring, ring))
            else:
                far_low[e] = Copy(FAR_LOW + f, [ends, ends], (True, True))
                far_high[e] = Copy(FAR_HIGH + f, [ends_high, ends_high], (True, True))
                if e in (0, "new"):
                    t = RELAY + 3 + (2 if e == "new" else 0)
                    relays["low", e] = Copy(FAR_LOW + f, [(to_low, to_low, partner), None], (False, False), t)
                    relays["high", e] = Copy(FAR_HIGH + f, [(to_high, to_high, partner), None], (False, False), t + 1)
        late = [] if prefill else [1, 2, 3]
        pair = remote(PAIR, fresh_ref, fresh_all.at[0, me], partner)

        def tiles(slot, part):
            return q_all.at[pl.ds(slot * TILES + part * 2, 2)]

        own_query = [q_ref.at[pl.ds(0, 2)], q_ref.at[pl.ds(2, 2)]]
        queries = [
            remote(QUERY, own_query[0], tiles(1, 0), q_right),
            remote(QUERY + 1, own_query[1], tiles(2, 1), q_left),
            remote(QUERY + 2, own_query[1], tiles(1, 1), q_right),
            remote(QUERY + 3, own_query[0], tiles(2, 0), q_left),
            remote(QUERY + 4, tiles(1, 0), tiles(3, 0), q_right),
            remote(QUERY + 5, tiles(2, 1), tiles(3, 1), q_left),
        ]

        def hand_on(received, onward):
            received.wait_recv()
            onward.start()

        def decode_row(slot, tile):
            return row_block(slot) * (ROWS // STEPS) + tile * (TILE // STEPS)

        def tile_episode(slot, tile):
            return 0 if prefill else episode_ref[decode_row(slot, tile)]

        def compute(items, where, first=False):
            all_scores, all_values = [], []
            for i in items:
                slot, tile = i // TILES, i % TILES
                if i < MAIN:
                    query, episode = q_all[i], tile_episode(slot, tile)
                else:
                    query, episode = q_all[extra_tile[i - MAIN]], i - MAIN + 1
                parts, values = [], []
                for b in where:
                    if b == "new":
                        if prefill:
                            limit = row_block(slot) * ROWS + tile * TILE + lane_position
                        else:
                            limit = jnp.where(episode == 0, 2 * STRETCH, -1)
                        s = scores(fresh_all[:, :, :, 0:DIM].reshape(RING * 2 * NEW, DIM), query)
                        kept = []
                        for part in range(2 * RING):
                            base = part % 2 * STRETCH + blocks[part // 2] * NEW
                            kept.append(jnp.where(new_row <= limit - base, s[part * NEW:(part + 1) * NEW], MASKED))
                        parts.append(jnp.concatenate(kept, axis=0))
                        values.append(fresh_all[:, :, :, DIM:2 * DIM].reshape(RING * 2 * NEW, DIM))
                    elif isinstance(b, str):
                        t = 0 if b == "new0" else 1
                        limit = row_block(slot) * ROWS + tile * TILE + lane_position
                        s = scores(fresh_all[:, t, :, 0:DIM].reshape(RING * NEW, DIM), query)
                        kept = []
                        for part in range(RING):
                            base = t * STRETCH + blocks[part] * NEW
                            kept.append(jnp.where(new_row <= limit - base, s[part * NEW:(part + 1) * NEW], MASKED))
                        parts.append(jnp.concatenate(kept, axis=0))
                        values.append(fresh_all[:, t, :, DIM:2 * DIM].reshape(RING * NEW, DIM))
                    else:
                        allowed = slot_row < len_ref[episode] - blocks[b] * SLOTS
                        parts.append(jnp.where(allowed, scores(buffers[b][episode, :, 0:DIM], query), MASKED))
                        values.append(buffers[b][episode, :, DIM:2 * DIM])
                all_scores.append(parts)
                all_values.append(values)
            update(items, all_scores, all_values, first)

        def state(slot, tile):
            i = slot * TILES + tile
            top, total, summed = acc_s[i, 0:1], acc_s[i, 1:2], acc_o[i]
            if prefill:
                return top, total, summed
            first = tile_episode(slot, tile)
            row_episode = jnp.zeros((1, LANES), jnp.int32)
            for r in range(TILE // STEPS):
                row_episode = jnp.where(
                    lane_position // STEPS == r, episode_ref[decode_row(slot, tile) + r], row_episode
                )
            for j in range(EXTRA):
                other = (row_episode == j + 1) & (first != j + 1)
                top = jnp.where(other, acc_s[MAIN + j, 0:1], top)
                total = jnp.where(other, acc_s[MAIN + j, 1:2], total)
                summed = jnp.where(other, acc_o[MAIN + j], summed)
            return top, total, summed

        def result(number, slot, part, into_o, into_s, device):
            n = (slot - 1) * 2 + part
            return (
                remote(RESULT + 2 * number, tx_o.at[n], into_o, device),
                remote(RESULT + 2 * number + 1, tx_s.at[n], into_s, device),
            )

        results = [
            result(0, 3, 0, mid_o.at[0], mid_s.at[0], q_right),
            result(1, 3, 1, mid_o.at[1], mid_s.at[1], q_left),
            result(2, 2, 1, fin_o.at[0, 1], fin_s.at[0, 1], q_right),
            result(3, 1, 0, fin_o.at[1, 0], fin_s.at[1, 0], q_left),
            result(4, 2, 0, fin_o.at[0, 0], fin_s.at[0, 0], q_right),
            result(5, 1, 1, fin_o.at[1, 1], fin_s.at[1, 1], q_left),
        ]

        def pack(slot, part, incoming=None):
            n = (slot - 1) * 2 + part
            for t in range(2):
                now = state(slot, part * 2 + t)
                if incoming is not None:
                    now = merge(now, load(mid_o.at[incoming], mid_s.at[incoming], t))
                tx_s[n, 2 * t:2 * t + 1] = now[0]
                tx_s[n, 2 * t + 1:2 * t + 2] = now[1]
                tx_o[n, t] = now[2].astype(jnp.bfloat16)

        def ship(number):
            for copy in results[number]:
                copy.start()

        def arrive(number):
            for copy in results[number]:
                copy.wait_recv()

        def settle():
            for copy in local_copies:
                copy.wait()
            tx_s[...] = jnp.zeros_like(tx_s)

        if prefill:
            settle()
        pair.start()
        for h in range(2):
            from_right[0, h].start()
            from_left[0, 1 - h].start()
        for copy in queries[:4]:
            copy.start()
        if not prefill:
            settle()
        if not prefill:
            for j in range(EXTRA):
                extra_tile[j] = 0
            for slot in range(RING):
                for tile in range(TILES):
                    low = tile_episode(slot, tile)
                    high = episode_ref[decode_row(slot, tile) + TILE // STEPS - 1]
                    for j in range(EXTRA):
                        hit = (low < j + 1) & (high >= j + 1)
                        extra_tile[j] = jnp.where(hit, slot * TILES + tile, extra_tile[j])
        compute(span(0, 4), [0], True)
        pair.wait_recv()
        from_right["new"].start()
        from_left["new"].start()

        def send(h, *episodes):
            for e in episodes:
                from_right[e, h].start()
                if not prefill:
                    from_left[e, 1 - h].start()

        def pass_on(side, key, *onward):
            {"right": from_right, "left": from_left, "low": far_low, "high": far_high}[side][key].wait_recv()
            if (side, key) in relays:
                relays[side, key].start()
            for copy in onward:
                copy.start()

        send(0, 1, 2, 3)
        if prefill:
            send(1, 1, 2, 3)
        hand_on(queries[0], queries[4])
        hand_on(queries[1], queries[5])
        pass_on("right", (0, 0), far_low[0])
        pass_on("left", (0, 1), far_high[0])
        if not prefill:
            send(1, 1)
        pass_on("right", (0, 1))
        pass_on("left", (0, 0))
        pass_on("right", "new", far_low["new"])
        pass_on("left", "new", far_high["new"])
        if not prefill:
            send(1, 2, 3)
        queries[2].wait_recv()
        queries[3].wait_recv()
        compute(span(4, 12), [0], True)
        if prefill:
            compute(span(0, 12), [1, 2])
            queries[4].wait_recv()
            queries[5].wait_recv()
            compute(span(12, 16), [0, 1, 2], True)
            for e in (0, "new"):
                far_low[e].wait_recv()
                far_high[e].wait_recv()
            last = ["new0", 3]

            def second(*slots):
                for slot in slots:
                    pl.when(row_block(slot) * ROWS >= STRETCH)(
                        functools.partial(compute, span(slot * TILES, slot * TILES + TILES), ["new1"]))

            compute(span(12, 16), last)
            second(3)
        else:
            for e in late:
                pass_on("right", (e, 0), far_low[e])
                pass_on("left", (e, 1), far_high[e])
            pass_on("low", 0)
            pass_on("high", 0)
            queries[4].wait_recv()
            queries[5].wait_recv()
            compute(span(12, 19), [0], True)
            pass_on("low", "new")
            pass_on("high", "new")
            compute(span(0, 8), ["new"])
            compute(span(8, 16), ["new"])
            for e in late:
                from_right[e, 1].wait_recv()
                from_left[e, 0].wait_recv()
            compute(span(0, 10), [1, 2])
            compute(span(10, 19), [1, 2])
            for e in late:
                far_low[e].wait_recv()
                far_high[e].wait_recv()
            last = [3]
            compute(span(12, 19), last)
        pack(3, 0)
        ship(0)
        pack(3, 1)
        ship(1)
        if prefill:
            compute(span(8, 12), last)
            second(2)
            pack(2, 1)
            ship(2)
            compute(span(4, 8), last)
            second(1)
        else:
            compute(span(4, 12), last)
            pack(2, 1)
            ship(2)
        pack(1, 0)
        ship(3)
        arrive(0)
        pack(2, 0, 0)
        ship(4)
        arrive(1)
        pack(1, 1, 1)
        ship(5)
        compute(span(0, 4), last)
        if prefill:
            second(0)

        for number in (2, 3, 4, 5):
            arrive(number)
        for tile in range(TILES):
            now = state(0, tile)
            for side in range(2):
                now = merge(now, load(fin_o.at[side, tile // 2], fin_s.at[side, tile // 2], tile % 2))
            whole = (now[2] * (1.0 / now[1])).T.astype(jnp.bfloat16)
            for h in range(HEADS):
                out_ref[tile, :, h * DIM:(h + 1) * DIM] = whole[h * TILE:(h + 1) * TILE]

        sent = [pair] + queries + [c for both in results for c in both]
        for table in (from_right, from_left, far_low, far_high, relays):
            sent += list(table.values())
        for copy in sent:
            copy.wait_send()

    @pl.when(grp == 0)
    def _():
        program(True)

    @pl.when(grp == 1)
    def _():
        program(False)


def local(queries, history_cache, fresh_cache, hist_len, decode_episode):
    vmem = pl.BlockSpec(memory_space=pltpu.VMEM)
    bf16, f32 = jnp.bfloat16, jnp.float32
    block = pltpu.VMEM((EPISODES, SLOTS, 2 * DIM), bf16)
    out = pl.pallas_call(
        kernel,
        out_shape=jax.ShapeDtypeStruct((TILES, TILE, HEADS * DIM), bf16),
        in_specs=[pl.BlockSpec(memory_space=pl.ANY)] * 5,
        out_specs=vmem,
        scratch_shapes=[
            pltpu.SMEM((EPISODES,), jnp.int32),
            pltpu.SMEM((512,), jnp.int32),
            block,
            block,
            block,
            block,
            pltpu.VMEM((RING, 2, NEW, 2 * DIM), bf16),
            pltpu.VMEM((MAIN, TILE, HEADS * DIM), bf16),
            pltpu.VMEM((MAIN + EXTRA, DIM, LANES), f32),
            pltpu.VMEM((MAIN + EXTRA, 8, LANES), f32),
            pltpu.VMEM((6, 2, DIM, LANES), bf16),
            pltpu.VMEM((6, 8, LANES), f32),
            pltpu.VMEM((2, 2, DIM, LANES), bf16),
            pltpu.VMEM((2, 8, LANES), f32),
            pltpu.VMEM((2, 2, 2, DIM, LANES), bf16),
            pltpu.VMEM((2, 2, 8, LANES), f32),
            pltpu.SMEM((EXTRA,), jnp.int32),
            pltpu.SemaphoreType.DMA((COPIES,)),
            pltpu.SemaphoreType.DMA((COPIES,)),
            pltpu.SemaphoreType.DMA((5,)),
        ],
        compiler_params=pltpu.CompilerParams(
            collective_id=0, has_side_effects=True, vmem_limit_bytes=56 * 1024 * 1024
        ),
    )(
        queries.reshape(TILES, TILE, HEADS * DIM),
        history_cache.reshape(EPISODES, SLOTS, 2 * DIM),
        fresh_cache.reshape(NEW, 2 * DIM),
        hist_len,
        decode_episode,
    )
    return out.reshape(1, ROWS, HEADS * DIM)


def solution(mesh):
    placed = (
        P("grp", "ctx", "head"),
        P(None, "ctx", "head", None),
        P("grp", "ctx", "head", None),
        P(),
        P(),
    )
    return jax.shard_map(
        local, mesh=mesh, in_specs=placed, out_specs=P("grp", "ctx", "head"), check_vma=False
    )
```
